256 devices in a mesh: tm: 2 (over core), space: 32 (over z, x), dp: 4 (over y).
Axes of the slice: x: 4, y: 4, z: 8, core: 2. Of those that a mesh axis runs over, the one named last changes fastest.
Arguments:
- features: bfloat16 [4, 6, 64, 104, 384], P('dp', 'tm', 'space'), may hold values from -6 to 6
- frame_index: int32 [4, 6], P('dp', 'tm'), may hold values from 0 to 15, as said below
- conv_weight: bfloat16 [10368, 384], P('dp'), may hold values from -0.0625 to 0.0625
- conv_bias: float32 [384], replicated, may hold values from -3 to 3
- norm_gain: float32 [384], replicated, may hold values from 0.25 to 1.75
- attn_gain: float32 [384], replicated, may hold values from 0.25 to 1.75
- qkv_weight: bfloat16 [384, 1152], P('dp'), may hold values from -2 to 2
- out_weight: bfloat16 [384, 384], P('dp'), may hold values from -0.3125 to 0.3125
Outputs:
- decoded: bfloat16 [4, 6, 64, 104, 384], P('dp', 'tm', 'space')
The draws below stay inside these ranges and needn't reach their ends.
Inputs may be any that keep to these rules, and one draw needn't show every extreme that they name: Along f, frame_index rises by one within a video and restarts at 0 where a new video begins; every video spans 9 to 16 frames, of which the slots may hold only a tail or a head.
All inputs are finite; a program needn't handle non-finite values.
Results may differ from the reference program's by a relative error of at most 0.029.
Values may be sent and summed in bfloat16 or wider, within the bound.
A program may use at most 192 MiB of HBM per device.

```python
import jax
import jax.numpy as jnp
from jax import lax

C = 384
W = 104
FRAMES = 6
STREAMS = 4
H = 64


def draw_frame_index(key, part):
    key = jax.random.fold_in(key, 7)
    runs = FRAMES // 9 + 3

    def one_stream(stream_key, stream):
        span_key, offset_key = jax.random.split(stream_key)
        spans = jax.random.randint(span_key, (runs,), 9, 17, dtype=jnp.int32)
        spans = jnp.where(jnp.logical_and(stream == 0, jnp.arange(runs) == 0), 16, spans).astype(jnp.int32)
        offset = jax.random.randint(offset_key, (), 0, 16, dtype=jnp.int32) % spans[0]
        offset = jnp.where(stream == 0, 15, offset).astype(jnp.int32)
        ends = jnp.cumsum(spans).astype(jnp.int32)
        starts = ends - spans
        slots = jnp.arange(FRAMES, dtype=jnp.int32) + offset
        began = starts[None, :] <= slots[:, None]
        run_start = jnp.max(jnp.where(began, starts[None, :], 0), axis=1)
        return (slots - run_start).astype(jnp.int32)
    stream_keys = jax.random.split(key, STREAMS)
    return jax.vmap(one_stream)(stream_keys, jnp.arange(STREAMS, dtype=jnp.int32)).astype(jnp.int32)


def draw_qkv_weight(key, part):
    key = jax.random.fold_in(key, 11)
    noise_key = jax.random.fold_in(key, 0)
    spread = float(C // 4) ** (-0.5)
    noise = jax.random.truncated_normal(noise_key, -4.0, 4.0, (C, 3 * C), jnp.float32) * spread
    return noise.astype(jnp.bfloat16)


def level_of(rng, extent, cuts, least, top_value):
    def one(dim, parts):
        heights = jax.random.uniform(jax.random.fold_in(jax.random.fold_in(rng, 6), dim), (parts,), jnp.float32, least / len(cuts), top_value / len(cuts))
        return jnp.repeat(jnp.exp(heights), extent[dim] // parts).reshape((-1,) + (1,) * (len(extent) - dim - 1))

    factor_of = one(*cuts[0])
    for cut in cuts[1:]:
        factor_of = factor_of * one(*cut)
    return factor_of


def bell_draw(own_key, extent, scale, bound, cuts=(), held_as=jnp.bfloat16):
    values = scale * jax.random.normal(own_key, extent, jnp.float32)
    if cuts:
        values = values * level_of(own_key, extent, cuts, -0.22, 0.18)
    return jnp.clip(values, -bound, bound).astype(held_as)


def setup_inputs(seed: int = 0) -> dict:
    streams_of = jax.random.split(jax.random.key(seed), 9)
    return {
        "features": bell_draw(streams_of[0], (STREAMS, FRAMES, H, W, C), 1.0, 6.0, ((0, 4), (1, 2), (2, 32))),
        "frame_index": draw_frame_index(jax.random.fold_in(streams_of[8], 71), 0),
        "conv_weight": bell_draw(streams_of[2], (27 * C, C), (27 * C) ** -0.5, 0.0625, ((0, 4),)),
        "conv_bias": bell_draw(streams_of[3], (C,), 0.3, 3.0, (), jnp.float32),
        "norm_gain": jnp.clip(1.0 + 0.15 * jax.random.normal(streams_of[4], (C,), jnp.float32), 0.25, 1.75),
        "attn_gain": jnp.clip(1.0 + 0.15 * jax.random.normal(streams_of[5], (C,), jnp.float32), 0.25, 1.75),
        "qkv_weight": draw_qkv_weight(jax.random.fold_in(streams_of[8], 71), 0),
        "out_weight": bell_draw(streams_of[7], (C, C), C ** -0.5, 0.3125, ((0, 4),)),
    }


EPS = 1e-06

def rms_scale(values, gain):
    values = values.astype(jnp.float32)
    return values * lax.rsqrt(lax.optimization_barrier(jnp.mean(values * values, axis=-1, keepdims=True)) + EPS) * gain

def reference(features, frame_index, conv_weight, conv_bias, norm_gain, attn_gain, qkv_weight, out_weight):
    chans = C
    kernel = conv_weight.reshape(3, 3, 3, chans, chans)
    activated = jax.nn.silu(rms_scale(features, norm_gain)).astype(jnp.bfloat16)
    padded = jnp.pad(activated, ((0, 0), (0, 0), (1, 1), (1, 1), (0, 0)))
    scale = 1.0 / jnp.sqrt(jnp.float32(chans))

    def one_frame(flat):
        stream = flat // FRAMES
        frame = flat % FRAMES
        position = frame_index[stream, frame]
        current = padded[stream, frame]
        keep_one = jnp.logical_and(position >= 1, frame >= 1).astype(jnp.bfloat16)
        keep_two = jnp.logical_and(position >= 2, frame >= 2).astype(jnp.bfloat16)
        earlier = padded[stream, jnp.maximum(frame - 1, 0)] * keep_one
        oldest = padded[stream, jnp.maximum(frame - 2, 0)] * keep_two
        conv = jnp.zeros((H * W, chans), jnp.float32)
        for tap_t, source in enumerate((oldest, earlier, current)):
            for tap_h in range(3):
                for tap_w in range(3):
                    window = source[tap_h:tap_h + H, tap_w:tap_w + W, :].reshape(H * W, chans)
                    conv = conv + jnp.dot(window, kernel[tap_t, tap_h, tap_w], preferred_element_type=jnp.float32)
        base = features[stream, frame].reshape(H * W, chans).astype(jnp.float32)
        hidden = (base + conv + conv_bias).astype(jnp.bfloat16)
        normed = rms_scale(hidden, attn_gain).astype(jnp.bfloat16)
        projected = jnp.dot(normed, qkv_weight, preferred_element_type=jnp.float32).astype(jnp.bfloat16)
        query = projected[:, :chans]
        keys = projected[:, chans:2 * chans]
        values = projected[:, 2 * chans:]
        scores = lax.dot_general(query, keys, (((1,), (1,)), ((), ())), preferred_element_type=jnp.float32) * scale
        shifted = jnp.exp(scores - lax.optimization_barrier(jnp.max(scores, axis=-1, keepdims=True)))
        probs = (shifted / lax.optimization_barrier(jnp.sum(shifted, axis=-1, keepdims=True))).astype(jnp.bfloat16)
        attended = jnp.dot(probs, values, preferred_element_type=jnp.float32).astype(jnp.bfloat16)
        result = hidden.astype(jnp.float32) + jnp.dot(attended, out_weight, preferred_element_type=jnp.float32)
        return result.astype(jnp.bfloat16).reshape(H, W, chans)
    frames_out = lax.map(one_frame, jnp.arange(STREAMS * FRAMES, dtype=jnp.int32))
    return frames_out.reshape(STREAMS, FRAMES, H, W, C)
```

```python
import functools
import math

import jax
import jax.numpy as jnp
from jax import lax
from jax.experimental import pallas as pl
from jax.experimental.pallas import tpu as pltpu
from jax.sharding import PartitionSpec as P

EPS = 1e-06
MESH = pl.DeviceIdType.MESH
XS = 4
ZS = 8
BF = jnp.bfloat16
F32 = jnp.float32


def with_halo(cells, sides, width):
    for axis, dim in sides:
        count = lax.axis_size(axis)
        ends = count - 1
        head = lax.slice_in_dim(cells, 0, width, axis=dim)
        tail = lax.slice_in_dim(cells, cells.shape[dim] - width, cells.shape[dim], axis=dim)
        cells = jnp.concatenate(
            [
                lax.ppermute(tail, axis, [(i, (i + 1) % count) for i in range(ends)]),
                cells,
                lax.ppermute(head, axis, [((i + 1) % count, i) for i in range(ends)]),
            ],
            axis=dim,
        )
    return cells


def passed_along(value, axis, steps):
    count = lax.axis_size(axis)
    first, last = (max(0, -steps), min(count, count - steps))
    return lax.ppermute(value, axis, [(source, source + steps) for source in range(first, last)])


def rms_scale(values, gain):
    values = values.astype(jnp.float32)
    return values * lax.rsqrt(jnp.mean(values * values, axis=-1, keepdims=True) + EPS) * gain


def build_patches(sources, rows, width):
    windows = []
    for source in sources:
        for tap_h in range(3):
            for tap_w in range(3):
                windows.append(source[:, tap_h : tap_h + rows, tap_w : tap_w + width, :])
    joined = jnp.concatenate(windows, axis=-1)
    return joined.reshape(-1, joined.shape[-1])


def dot(a, b):
    return jnp.dot(a, b, preferred_element_type=F32)


def dot_t(a, b):
    return lax.dot_general(a, b, (((1,), (1,)), ((), ())), preferred_element_type=F32)


def attention_kernel(
    hid, qkv, outw, gain, out,
    nbuf, kb, qbuf, mbuf, lbuf, acc, obuf, rbuf,
    home_send, ret_send, sib_send, left_send, right_send, on_send, recv, ret_recv,
):
    chans = hid.shape[-1]
    t = lax.axis_index("tm")
    space = lax.axis_index("space")
    z, x = lax.div(space, XS), lax.rem(space, XS)
    left, right, across = lax.rem(x + XS - 1, XS), lax.rem(x + 1, XS), lax.rem(x + 2, XS)
    parity = lax.rem(z, 2)
    same = t == parity

    def dev(core, row, col):
        return {"tm": core, "space": row * XS + col}

    barrier = pltpu.get_barrier_semaphore()

    def greet(core, row, col):
        pl.semaphore_signal(barrier, inc=1, device_id=dev(core, row, col), device_id_type=MESH)

    greet(1 - t, z, x)
    greet(t, z, left)
    greet(t, z, right)
    for d in range(1, ZS):
        for core in range(2):
            greet(core, lax.rem(z + d, ZS), x)

    for j in range(3):
        nbuf[j] = rms_scale(hid[j], gain[...]).astype(BF)

    pl.semaphore_wait(barrier, 3 + 2 * (ZS - 1))

    def copy(src, dst, send, rec, device):
        return pltpu.make_async_remote_copy(
            src_ref=src, dst_ref=dst, send_sem=send, recv_sem=rec, device_id=device, device_id_type=MESH
        )

    def home_copy(j):
        b = x * ZS + z
        return copy(nbuf.at[j], kb.at[b], home_send.at[j], recv.at[b], dev(parity, 2 * j + t, x))

    for j in range(3):
        @pl.when(2 * j + t != z)
        def _():
            home_copy(j).start()

    is_worker = z < 6

    @pl.when(is_worker)
    def _():
        slot = lax.div(z, 2)

        def row_of(i, mine):
            first = jnp.where(same, (0, 2, 6, 4)[i], (1, 7, 3, 5)[i])
            second = jnp.where(same, (1, 7, 3, 5)[i], (0, 2, 6, 4)[i])
            return lax.rem(z + (first if mine else second), ZS)

        def block(col, i, mine=True):
            return col * ZS + row_of(i, mine)

        def landed(b):
            copy(kb.at[b], kb.at[b], sib_send.at[0], recv.at[b], dev(1 - t, z, x)).wait_recv()

        def push(b, send, device):
            return copy(kb.at[b], kb.at[b], send, recv.at[b], device)

        sib, lft, rgt = dev(1 - t, z, x), dev(t, z, left), dev(t, z, right)
        sent = []

        def own(i):
            b = block(x, i)
            if i == 0:
                @pl.when(same)
                def _():
                    kb[b] = nbuf[slot]

                @pl.when(jnp.logical_not(same))
                def _():
                    landed(b)
            else:
                landed(b)
            for c in (push(b, left_send.at[i], lft), push(b, right_send.at[i], rgt), push(b, sib_send.at[i], sib)):
                c.start()
                sent.append(c)

        def beside(i):
            for k, (col, on) in enumerate(((left, rgt), (right, lft))):
                b = block(col, i)
                landed(b)
                if (i < 2) == (k == 0):
                    c = push(b, on_send.at[i], on)
                    c.start()
                    sent.append(c)
                c = push(b, sib_send.at[4 + 2 * i + k], sib)
                c.start()
                sent.append(c)

        def far(i):
            b = block(across, i)
            landed(b)
            c = push(b, sib_send.at[12 + i], sib)
            c.start()
            sent.append(c)

        def others(col):
            for i in range(4):
                landed(block(col, i, False))

        def project(i):
            n = kb[block(x, i)]
            q = dot(n, qkv[:, :chans]).astype(BF)
            qk = dot_t(q, qkv[:, chans : 2 * chans]) * (math.log2(math.e) / math.sqrt(chans))
            qbuf[i] = qk.astype(BF)

        def attend(i, col, first):
            keys = kb[pl.ds(col * ZS, ZS)].reshape(-1, chans)
            s = dot_t(qbuf[i], keys)
            top = jnp.max(s, axis=-1, keepdims=True)
            if not first:
                top = jnp.maximum(top, mbuf[i])
            p = jnp.exp2(s - top)
            total = jnp.sum(p, axis=-1, keepdims=True)
            mixed = dot(p.astype(BF), keys)
            if not first:
                alpha = jnp.exp2(mbuf[i] - top)
                total = total + lbuf[i] * alpha
                mixed = mixed + acc[i] * alpha
            mbuf[i] = top
            lbuf[i] = total
            acc[i] = mixed

        def back(i):
            return copy(
                obuf.at[i], rbuf.at[slot], ret_send.at[i], ret_recv.at[slot], dev(parity, row_of(i, True), x)
            )

        def finish(i):
            mixed = (acc[i] * (1.0 / lbuf[i])).astype(BF)
            attended = dot(mixed, qkv[:, 2 * chans :]).astype(BF)
            if i == 0:
                @pl.when(same)
                def _():
                    rbuf[slot] = attended

                @pl.when(jnp.logical_not(same))
                def _():
                    obuf[i] = attended
                    back(i).start()
            else:
                obuf[i] = attended
                back(i).start()

        own(0)
        own(1)
        beside(0)
        own(2)
        beside(1)
        own(3)
        for i in range(4):
            project(i)
        others(x)
        attend(0, x, True)
        beside(2)
        attend(1, x, True)
        beside(3)
        attend(2, x, True)
        far(0)
        attend(3, x, True)
        others(left)
        attend(0, left, False)
        far(1)
        attend(1, left, False)
        attend(2, left, False)
        far(2)
        attend(3, left, False)
        others(right)
        attend(0, right, False)
        far(3)
        for i in range(1, 4):
            attend(i, right, False)
        others(across)
        for i in range(4):
            attend(i, across, False)
            finish(i)
        for c in sent:
            c.wait_send()
        for i in range(4):
            if i == 0:
                @pl.when(jnp.logical_not(same))
                def _():
                    back(i).wait_send()
            else:
                back(i).wait_send()

    for j in range(3):
        @pl.when(2 * j + t != z)
        def _():
            home_copy(j).wait_send()
            copy(rbuf.at[j], rbuf.at[j], ret_send.at[0], ret_recv.at[j], dev(1 - t, z, x)).wait_recv()

        out[j] = (hid[j].astype(F32) + dot(rbuf[j], outw[...])).astype(BF)


def attention(hidden, qkv, outw, gain):
    frames, pixels, chans = hidden.shape
    vmem = pl.BlockSpec(memory_space=pltpu.VMEM)
    dma = pltpu.SemaphoreType.DMA
    return pl.pallas_call(
        attention_kernel,
        out_shape=jax.ShapeDtypeStruct(hidden.shape, BF),
        in_specs=[vmem] * 4,
        out_specs=vmem,
        scratch_shapes=[
            pltpu.VMEM((3, pixels, chans), BF),
            pltpu.VMEM((XS * ZS, pixels, chans), BF),
            pltpu.VMEM((4, pixels, chans), BF),
            pltpu.VMEM((4, pixels, 1), F32),
            pltpu.VMEM((4, pixels, 1), F32),
            pltpu.VMEM((4, pixels, chans), F32),
            pltpu.VMEM((4, pixels, chans), BF),
            pltpu.VMEM((3, pixels, chans), BF),
            dma((3,)), dma((4,)), dma((16,)), dma((4,)), dma((4,)), dma((4,)),
            dma((XS * ZS,)), dma((3,)),
        ],
        compiler_params=pltpu.CompilerParams(
            collective_id=1, has_side_effects=True, vmem_limit_bytes=48 * 1024 * 1024
        ),
        cost_estimate=pl.CostEstimate(
            flops=4 * 4 * pixels * 32 * pixels * chans, bytes_accessed=4 * frames * pixels * chans,
            transcendentals=4 * pixels * 32 * pixels,
        ),
    )(hidden, qkv, outw, gain.reshape(1, chans))


def on_device(
    features, frame_index, conv_weight, conv_bias, norm_gain, attn_gain, qkv_weight, out_weight
):
    frames, rows, width, chans = (
        features.shape[1],
        features.shape[2],
        features.shape[3],
        features.shape[4],
    )
    pixels = rows * width
    full_qkv, full_out = (
        lax.all_gather(qkv_weight, "dp", axis=0, tiled=True),
        lax.all_gather(out_weight, "dp", axis=0, tiled=True),
    )
    local = features[0]
    activated = jax.nn.silu(rms_scale(local, norm_gain)).astype(jnp.bfloat16)
    rimmed = with_halo(activated, (("space", 1),), 1)
    rimmed = jnp.pad(rimmed, ((0, 0), (0, 0), (1, 1), (0, 0)))
    prior = passed_along(rimmed[frames - 2 :], "tm", 1)
    sequence = jnp.concatenate([prior, rimmed], axis=0)
    position = frame_index[0]
    keep_one = (position >= 1).astype(jnp.bfloat16)[:, None, None, None]
    keep_two = (position >= 2).astype(jnp.bfloat16)[:, None, None, None]
    earlier = sequence[1 : frames + 1] * keep_one
    oldest = sequence[:frames] * keep_two
    patches = build_patches((oldest, earlier, rimmed), rows, width)
    conv = jnp.dot(
        patches,
        lax.all_gather(conv_weight, "dp", axis=0, tiled=True),
        preferred_element_type=jnp.float32,
    )
    hidden = (local.reshape(frames * pixels, chans).astype(jnp.float32) + conv + conv_bias).astype(
        jnp.bfloat16
    )
    result = attention(hidden.reshape(frames, pixels, chans), full_qkv, full_out, attn_gain)
    return result.reshape(1, frames, rows, width, chans)


def solution(mesh):
    placed = (
        P("dp", "tm", "space", None, None),
        P("dp", "tm"),
        P("dp", None),
        P(),
        P(),
        P(),
        P("dp", None),
        P("dp", None),
    )
    return jax.shard_map(
        on_device,
        mesh=mesh,
        in_specs=placed,
        out_specs=P("dp", "tm", "space", None, None),
        check_vma=False,
    )
```

```python
import functools
import math

import jax
import jax.numpy as jnp
from jax import lax
from jax.experimental import pallas as pl
from jax.experimental.pallas import tpu as pltpu
from jax.sharding import PartitionSpec as P

EPS = 1e-06
MESH = pl.DeviceIdType.MESH
XS = 4
ZS = 8
BF = jnp.bfloat16
F32 = jnp.float32


def rms_scale(values, gain):
    values = values.astype(jnp.float32)
    return values * lax.rsqrt(jnp.mean(values * values, axis=-1, keepdims=True) + EPS) * gain


def dot(a, b):
    return jnp.dot(a, b, preferred_element_type=F32)


def dot_t(a, b):
    return lax.dot_general(a, b, (((1,), (1,)), ((), ())), preferred_element_type=F32)


def attention_kernel(
    hid, qkv, outw, gain, out,
    nbuf, kb, qbuf, mbuf, lbuf, acc, obuf, rbuf,
    home_send, ret_send, sib_send, left_send, right_send, on_send, recv, ret_recv,
):
    chans = hid.shape[-1]
    t = lax.axis_index("tm")
    space = lax.axis_index("space")
    z, x = lax.div(space, XS), lax.rem(space, XS)
    left, right, across = lax.rem(x + XS - 1, XS), lax.rem(x + 1, XS), lax.rem(x + 2, XS)
    parity = lax.rem(z, 2)
    same = t == parity

    def dev(core, row, col):
        return {"tm": core, "space": row * XS + col}

    barrier = pltpu.get_barrier_semaphore()

    def greet(core, row, col):
        pl.semaphore_signal(barrier, inc=1, device_id=dev(core, row, col), device_id_type=MESH)

    greet(1 - t, z, x)
    greet(t, z, left)
    greet(t, z, right)
    for d in range(1, ZS):
        for core in range(2):
            greet(core, lax.rem(z + d, ZS), x)

    for j in range(3):
        nbuf[j] = rms_scale(hid[j], gain[...]).astype(BF)

    pl.semaphore_wait(barrier, 3 + 2 * (ZS - 1))

    def copy(src, dst, send, rec, device):
        return pltpu.make_async_remote_copy(
            src_ref=src, dst_ref=dst, send_sem=send, recv_sem=rec, device_id=device, device_id_type=MESH
        )

    def home_copy(j):
        b = x * ZS + z
        return copy(nbuf.at[j], kb.at[b], home_send.at[j], recv.at[b], dev(parity, 2 * j + t, x))

    for j in range(3):
        @pl.when(2 * j + t != z)
        def _():
            home_copy(j).start()

    is_worker = z < 6

    @pl.when(is_worker)
    def _():
        slot = lax.div(z, 2)

        def row_of(i, mine):
            first = jnp.where(same, (0, 2, 6, 4)[i], (1, 7, 3, 5)[i])
            second = jnp.where(same, (1, 7, 3, 5)[i], (0, 2, 6, 4)[i])
            return lax.rem(z + (first if mine else second), ZS)

        def block(col, i, mine=True):
            return col * ZS + row_of(i, mine)

        def landed(b):
            copy(kb.at[b], kb.at[b], sib_send.at[0], recv.at[b], dev(1 - t, z, x)).wait_recv()

        def push(b, send, device):
            return copy(kb.at[b], kb.at[b], send, recv.at[b], device)

        sib, lft, rgt = dev(1 - t, z, x), dev(t, z, left), dev(t, z, right)
        sent = []

        def own(i):
            b = block(x, i)
            if i == 0:
                @pl.when(same)
                def _():
                    kb[b] = nbuf[slot]

                @pl.when(jnp.logical_not(same))
                def _():
                    landed(b)
            else:
                landed(b)
            for c in (push(b, left_send.at[i], lft), push(b, right_send.at[i], rgt), push(b, sib_send.at[i], sib)):
                c.start()
                sent.append(c)

        def beside(i):
            for k, (col, on) in enumerate(((left, rgt), (right, lft))):
                b = block(col, i)
                landed(b)
                if (i < 2) == (k == 0):
                    c = push(b, on_send.at[i], on)
                    c.start()
                    sent.append(c)
                c = push(b, sib_send.at[4 + 2 * i + k], sib)
                c.start()
                sent.append(c)

        def far(i):
            b = block(across, i)
            landed(b)
            c = push(b, sib_send.at[12 + i], sib)
            c.start()
            sent.append(c)

        def others(col):
            for i in range(4):
                landed(block(col, i, False))

        def project(i):
            n = kb[block(x, i)]
            q = dot(n, qkv[:, :chans]).astype(BF)
            qk = dot_t(q, qkv[:, chans : 2 * chans]) * (math.log2(math.e) / math.sqrt(chans))
            qbuf[i] = qk.astype(BF)

        def attend(i, col, first):
            keys = kb[pl.ds(col * ZS, ZS)].reshape(-1, chans)
            s = dot_t(qbuf[i], keys)
            top = jnp.max(s, axis=-1, keepdims=True)
            if not first:
                top = jnp.maximum(top, mbuf[i])
            p = jnp.exp2(s - top)
            total = jnp.sum(p, axis=-1, keepdims=True)
            mixed = dot(p.astype(BF), keys)
            if not first:
                alpha = jnp.exp2(mbuf[i] - top)
                total = total + lbuf[i] * alpha
                mixed = mixed + acc[i] * alpha
            mbuf[i] = top
            lbuf[i] = total
            acc[i] = mixed

        def back(i):
            return copy(
                obuf.at[i], rbuf.at[slot], ret_send.at[i], ret_recv.at[slot], dev(parity, row_of(i, True), x)
            )

        def finish(i):
            mixed = (acc[i] * (1.0 / lbuf[i])).astype(BF)
            attended = dot(mixed, qkv[:, 2 * chans :]).astype(BF)
            if i == 0:
                @pl.when(same)
                def _():
                    rbuf[slot] = attended

                @pl.when(jnp.logical_not(same))
                def _():
                    obuf[i] = attended
                    back(i).start()
            else:
                obuf[i] = attended
                back(i).start()

        own(0)
        own(1)
        beside(0)
        own(2)
        beside(1)
        own(3)
        for i in range(4):
            project(i)
        others(x)
        attend(0, x, True)
        beside(2)
        attend(1, x, True)
        beside(3)
        attend(2, x, True)
        far(0)
        attend(3, x, True)
        others(left)
        attend(0, left, False)
        far(1)
        attend(1, left, False)
        attend(2, left, False)
        far(2)
        attend(3, left, False)
        others(right)
        attend(0, right, False)
        far(3)
        for i in range(1, 4):
            attend(i, right, False)
        others(across)
        for i in range(4):
            attend(i, across, False)
            finish(i)
        for c in sent:
            c.wait_send()
        for i in range(4):
            if i == 0:
                @pl.when(jnp.logical_not(same))
                def _():
                    back(i).wait_send()
            else:
                back(i).wait_send()

    for j in range(3):
        @pl.when(2 * j + t != z)
        def _():
            home_copy(j).wait_send()
            copy(rbuf.at[j], rbuf.at[j], ret_send.at[0], ret_recv.at[j], dev(1 - t, z, x)).wait_recv()

        out[j] = (hid[j].astype(F32) + dot(rbuf[j], outw[...])).astype(BF)


def attention(hidden, qkv, outw, gain):
    frames, pixels, chans = hidden.shape
    vmem = pl.BlockSpec(memory_space=pltpu.VMEM)
    dma = pltpu.SemaphoreType.DMA
    return pl.pallas_call(
        attention_kernel,
        out_shape=jax.ShapeDtypeStruct(hidden.shape, BF),
        in_specs=[vmem] * 4,
        out_specs=vmem,
        scratch_shapes=[
            pltpu.VMEM((3, pixels, chans), BF),
            pltpu.VMEM((XS * ZS, pixels, chans), BF),
            pltpu.VMEM((4, pixels, chans), BF),
            pltpu.VMEM((4, pixels, 1), F32),
            pltpu.VMEM((4, pixels, 1), F32),
            pltpu.VMEM((4, pixels, chans), F32),
            pltpu.VMEM((4, pixels, chans), BF),
            pltpu.VMEM((3, pixels, chans), BF),
            dma((3,)), dma((4,)), dma((16,)), dma((4,)), dma((4,)), dma((4,)),
            dma((XS * ZS,)), dma((3,)),
        ],
        compiler_params=pltpu.CompilerParams(
            collective_id=1, has_side_effects=True, vmem_limit_bytes=48 * 1024 * 1024
        ),
        cost_estimate=pl.CostEstimate(
            flops=4 * 4 * pixels * 32 * pixels * chans, bytes_accessed=4 * frames * pixels * chans,
            transcendentals=4 * pixels * 32 * pixels,
        ),
    )(hidden, qkv, outw, gain.reshape(1, chans))


QUARTER = 2592
HALF = 1280
PART = 640
XPIECE = PART // XS
ZPIECE = PART // ZS
REST = 16
WIDE = 112


def conv_kernel(
    feat, fidx, w, qkvw, ow, bias, gain, hid, qkv_out, ow_out,
    wb, qb, ob, u, lhs, acc,
    local_sem, y_send, y_recv, x_send, x_on, x_recv, z_send, z_on, z_recv, s_send, s_recv,
    h_send, h_recv,
):
    chans = feat.shape[-1]
    width = feat.shape[-2]
    t = lax.axis_index("tm")
    space = lax.axis_index("space")
    y = lax.axis_index("dp")
    z, x = lax.div(space, XS), lax.rem(space, XS)
    left, right, across = lax.rem(x + XS - 1, XS), lax.rem(x + 1, XS), lax.rem(x + 2, XS)
    down, up = lax.rem(z + ZS - 1, ZS), lax.rem(z + 1, ZS)
    before, after = lax.rem(space + 31, 32), lax.rem(space + 1, 32)

    def dev(core, row, col):
        return {"tm": core, "space": row * XS + col}

    sib, lft, rgt = dev(1 - t, z, x), dev(t, z, left), dev(t, z, right)
    dwn, upw = dev(t, down, x), dev(t, up, x)
    barrier = pltpu.get_barrier_semaphore()

    def greet(device):
        pl.semaphore_signal(barrier, inc=1, device_id=device, device_id_type=MESH)

    for d in range(1, 4):
        greet({"dp": lax.rem(y + d, 4)})
    for device in (sib, lft, rgt, dwn, upw):
        greet(device)
    for core in range(2):
        greet({"tm": core, "space": before})
        greet({"tm": core, "space": after})

    def copy(src, dst, send, rec, device):
        return pltpu.make_async_remote_copy(
            src_ref=src, dst_ref=dst, send_sem=send, recv_sem=rec, device_id=device, device_id_type=MESH
        )

    def rows(start, count):
        return pl.ds(pl.multiple_of(start, 16), count)

    mine = pltpu.make_async_copy(w, wb.at[rows(y * QUARTER, QUARTER)], local_sem)
    mine.start()

    pad = jnp.zeros((WIDE - width, chans), F32)
    for f in range(3):
        for r in range(2):
            scaled = rms_scale(feat[0, f, r], gain[...])
            act = scaled * jax.nn.sigmoid(scaled)
            u[1 + r, 2 + f] = jnp.concatenate([act, pad], axis=0).astype(BF)
    blank = jnp.zeros((3, WIDE, chans), BF)

    @pl.when(space == 0)
    def _():
        u[0, 2:5] = blank
        u[0, 0:2] = blank[:2]

    @pl.when(space == 31)
    def _():
        u[3, 2:5] = blank
        u[3, 0:2] = blank[:2]

    @pl.when(t == 0)
    def _():
        for r in range(4):
            u[r, 0:2] = blank[:2]

    pl.semaphore_wait(barrier, 12)

    sent = []

    def go(c):
        c.start()
        sent.append(c)

    def x_rows(j, col):
        return rows(j * QUARTER + t * HALF + col * XPIECE, XPIECE)

    def z_rows(j, row):
        return rows(j * QUARTER + t * HALF + PART + row * ZPIECE, ZPIECE)

    def rest_rows(j, core):
        return rows(j * QUARTER + 2 * HALF + core * REST, REST)

    def half_rows(core):
        return rows(core * 48, 48)

    owner = [lax.rem(y + d, 4) for d in (3, 1, 2)]
    target = [{"dp": lax.rem(y + d, 4)} for d in (1, 3, 2)]
    for k in range(3):
        src = w.at[rows(t * HALF + x * XPIECE, XPIECE)]
        go(copy(src, wb.at[x_rows(y, x)], y_send.at[k, 0], y_recv.at[k, 0], target[k]))
        src = w.at[rows(t * HALF + PART + z * ZPIECE, ZPIECE)]
        go(copy(src, wb.at[z_rows(y, z)], y_send.at[k, 1], y_recv.at[k, 1], target[k]))

    def rim(src, dst, n, device):
        return copy(src, dst, h_send.at[n], h_recv.at[n], device)

    rims = (
        (space < 31, rim(u.at[2, 2:5], u.at[0, 2:5], 0, {"space": after})),
        (space > 0, rim(u.at[1, 2:5], u.at[3, 2:5], 1, {"space": before})),
        (t == 0, rim(u.at[1:3, 3:5], u.at[1:3, 0:2], 2, {"tm": 1 - t})),
        (jnp.logical_and(t == 0, space < 31), rim(u.at[2, 3:5], u.at[0, 0:2], 3, {"tm": 1 - t, "space": after})),
        (jnp.logical_and(t == 0, space > 0), rim(u.at[1, 3:5], u.at[3, 0:2], 4, {"tm": 1 - t, "space": before})),
    )
    for cond, c in rims:
        pl.when(cond)(c.start)

    for k in range(3):
        src = w.at[rows(2 * HALF + t * REST, REST)]
        go(copy(src, wb.at[rest_rows(y, t)], y_send.at[k, 2], y_recv.at[k, 2], target[k]))
        go(copy(qkvw.at[half_rows(t)], qb.at[y, half_rows(t)], y_send.at[k, 3], y_recv.at[k, 3], target[k]))
        go(copy(ow.at[half_rows(t)], ob.at[y, half_rows(t)], y_send.at[k, 4], y_recv.at[k, 4], target[k]))

    def landed(ref, sem):
        copy(ref, ref, s_send.at[0, 0], sem, sib).wait_recv()

    def push(ref, send, rec, device):
        go(copy(ref, ref, send, rec, device))

    def from_y(k):
        ref = wb.at[x_rows(owner[k], x)]
        landed(ref, y_recv.at[k, 0])
        push(ref, x_send.at[k, 0], x_recv.at[k, 0], rgt)
        push(ref, x_send.at[k, 1], x_recv.at[k, 1], lft)
        ref = wb.at[z_rows(owner[k], z)]
        landed(ref, y_recv.at[k, 1])
        push(ref, z_send.at[k, 0], z_recv.at[k, 0], upw)
        push(ref, z_send.at[k, 1], z_recv.at[k, 1], dwn)

    def x_one(k):
        for way, (col, on) in enumerate(((left, rgt), (right, lft))):
            ref = wb.at[x_rows(owner[k], col)]
            landed(ref, x_recv.at[k, way])
            if way == k % 2:
                push(ref, x_on.at[k], x_recv.at[k, 2], on)

    def x_two(k):
        landed(wb.at[x_rows(owner[k], across)], x_recv.at[k, 2])
        push(wb.at[rows(owner[k] * QUARTER + t * HALF, PART)], s_send.at[k, 0], s_recv.at[k, 0], sib)

    def z_step(k, d):
        for way, on in enumerate((upw, dwn)):
            row = lax.rem(z + (ZS - d if way == 0 else d), ZS)
            ref = wb.at[z_rows(owner[k], row)]
            landed(ref, z_recv.at[k, 2 * d - 2 + way])
            if d < 3:
                push(ref, z_on.at[k, 2 * d - 2 + way], z_recv.at[k, 2 * d + way], on)
            elif way == k % 2:
                push(ref, z_on.at[k, 4], z_recv.at[k, 6], on)

    def z_last(k):
        landed(wb.at[z_rows(owner[k], lax.rem(z + 4, ZS))], z_recv.at[k, 6])
        push(wb.at[rows(owner[k] * QUARTER + t * HALF + PART, PART)], s_send.at[k, 1], s_recv.at[k, 1], sib)

    def small(k):
        for n, ref in enumerate(
            (wb.at[rest_rows(owner[k], t)], qb.at[owner[k], half_rows(t)], ob.at[owner[k], half_rows(t)])
        ):
            landed(ref, y_recv.at[k, 2 + n])
            push(ref, s_send.at[k, 2 + n], s_recv.at[k, 2 + n], sib)

    def shared(k):
        start = owner[k] * QUARTER + (1 - t) * HALF
        landed(wb.at[rows(start, PART)], s_recv.at[k, 0])
        landed(wb.at[rows(start + PART, PART)], s_recv.at[k, 1])
        landed(wb.at[rest_rows(owner[k], 1 - t)], s_recv.at[k, 2])

    keep = [
        [(fidx[0, f] >= 2 - kt).astype(F32) for f in range(3)] for kt in range(2)
    ]

    def spread(g, r):
        cells = u[r, g].astype(F32)
        for kw in range(3):
            moved = cells if kw == 1 else pltpu.roll(cells, 1 if kw == 0 else WIDE - 1, 0)
            for kt in range(3):
                f = g - kt
                if 0 <= f < 3:
                    lhs[kt * 3 + kw, f, r] = (moved if kt == 2 else moved * keep[kt][f]).astype(BF)

    def tap(number):
        kt, kh, kw = number // 9, (number // 3) % 3, number % 3
        if not isinstance(number, int):
            kt, kh, kw = lax.div(number, 9), lax.rem(lax.div(number, 3), 3), lax.rem(number, 3)
        cells = lhs[kt * 3 + kw, :, pl.ds(kh, 2)].reshape(-1, chans)
        acc[...] += dot(cells, wb[rows(number * chans, chans)])

    def taps(j, first, last):
        @pl.loop(first, last)
        def _(i):
            tap(7 * j + i)

    for g in range(2, 5):
        for r in range(1, 3):
            spread(g, r)
    from_y(0)
    from_y(1)
    x_one(0)
    z_step(0, 1)
    from_y(2)
    for n, cond in enumerate(
        (space > 0, space < 31, t == 1, jnp.logical_and(t == 1, space > 0), jnp.logical_and(t == 1, space < 31))
    ):
        pl.when(cond)(rims[n][1].wait_recv)
    for g in range(2, 5):
        spread(g, 0)
        spread(g, 3)
    z_step(0, 2)
    x_one(1)
    z_step(1, 1)
    for g in range(2):
        for r in range(4):
            spread(g, r)
    x_two(0)
    z_step(0, 3)
    z_step(1, 2)
    x_one(2)
    z_step(2, 1)
    acc[...] = jnp.zeros_like(acc)
    mine.wait()
    taps(y, 0, 2)
    x_two(1)
    z_last(0)
    z_step(1, 3)
    z_step(2, 2)
    taps(y, 2, 4)
    x_two(2)
    z_last(1)
    z_step(2, 3)
    taps(y, 4, 6)
    for k in range(3):
        small(k)
    z_last(2)
    for k in range(3):
        shared(k)
        taps(owner[k], 0, 6)
    for number in (6, 13, 20):
        tap(number)

    for f in range(3):
        both = []
        for r in range(2):
            part = acc[pl.ds((f * 2 + r) * WIDE, width)]
            both.append(feat[0, f, r].astype(F32) + part + bias[...])
        hid[f] = jnp.concatenate(both, axis=0).astype(BF)

    for k in range(3):
        landed(qb.at[owner[k], half_rows(1 - t)], s_recv.at[k, 3])
        landed(ob.at[owner[k], half_rows(1 - t)], s_recv.at[k, 4])
    for j in range(4):
        qkv_out[pl.ds(96 * j, 96)] = qb[j]
        ow_out[pl.ds(96 * j, 96)] = ob[j]
    mine_rows = rows(96 * y, 96)
    qkv_out[mine_rows] = qkvw[...]
    ow_out[mine_rows] = ow[...]

    for c in sent:
        c.wait_send()
    for cond, c in rims:
        pl.when(cond)(c.wait_send)


def convolution(feat, fidx, w, qkvw, ow, bias, gain):
    chans = feat.shape[-1]
    vmem = pl.BlockSpec(memory_space=pltpu.VMEM)
    smem = pl.BlockSpec(memory_space=pltpu.SMEM)
    hbm = pl.BlockSpec(memory_space=pl.ANY)
    dma = pltpu.SemaphoreType.DMA
    return pl.pallas_call(
        conv_kernel,
        out_shape=(
            jax.ShapeDtypeStruct((3, 208, chans), BF),
            jax.ShapeDtypeStruct((chans, 3 * chans), BF),
            jax.ShapeDtypeStruct((chans, chans), BF),
        ),
        in_specs=[vmem, smem, hbm, vmem, vmem, vmem, vmem],
        out_specs=(vmem,) * 3,
        scratch_shapes=[
            pltpu.VMEM((4 * QUARTER, chans), BF),
            pltpu.VMEM((4, 96, 3 * chans), BF),
            pltpu.VMEM((4, 96, chans), BF),
            pltpu.VMEM((4, 5, WIDE, chans), BF),
            pltpu.VMEM((9, 3, 4, WIDE, chans), BF),
            pltpu.VMEM((6 * WIDE, chans), F32),
            dma, dma((3, 5)), dma((3, 5)), dma((3, 2)), dma((3,)), dma((3, 3)),
            dma((3, 2)), dma((3, 5)), dma((3, 7)), dma((3, 5)), dma((3, 5)),
            dma((5,)), dma((5,)),
        ],
        compiler_params=pltpu.CompilerParams(
            collective_id=2, has_side_effects=True, vmem_limit_bytes=48 * 1024 * 1024
        ),
        cost_estimate=pl.CostEstimate(
            flops=2 * 624 * 27 * chans * chans, bytes_accessed=4 * QUARTER * chans * 2, transcendentals=0
        ),
    )(feat, fidx, w, qkvw, ow, bias.reshape(1, chans), gain.reshape(1, chans))


def on_device(
    features, frame_index, conv_weight, conv_bias, norm_gain, attn_gain, qkv_weight, out_weight
):
    hidden, full_qkv, full_out = convolution(
        features, frame_index, conv_weight, qkv_weight, out_weight, conv_bias, norm_gain
    )
    return attention(hidden, full_qkv, full_out, attn_gain).reshape(features.shape)


def solution(mesh):
    placed = (
        P("dp", "tm", "space", None, None),
        P("dp", "tm"),
        P("dp", None),
        P(),
        P(),
        P(),
        P("dp", None),
        P("dp", None),
    )
    return jax.shard_map(
        on_device,
        mesh=mesh,
        in_specs=placed,
        out_specs=P("dp", "tm", "space", None, None),
        check_vma=False,
    )
```

```python
import math

import jax
import jax.numpy as jnp
from jax import lax
from jax.experimental import pallas as pl
from jax.experimental.pallas import tpu as pltpu
from jax.sharding import PartitionSpec as P

EPS = 1e-06
MESH = pl.DeviceIdType.MESH
BF = jnp.bfloat16
F32 = jnp.float32
XS = 4
ZS = 8
YS = 4
QUARTER = 2592
HALF = 1280
XPIECE = HALF // XS
ZPIECE = HALF // ZS
REST = 16
WIDE = 112
CHUNKS = ((0, 48), (48, 48), (96, 48), (144, 64))


def rms_scale(values, gain):
    values = values.astype(F32)
    return values * lax.rsqrt(jnp.mean(values * values, axis=-1, keepdims=True) + EPS) * gain


def dot(a, b):
    return jnp.dot(a, b, preferred_element_type=F32)


def dot_t(a, b):
    return lax.dot_general(a, b, (((1,), (1,)), ((), ())), preferred_element_type=F32)


def kernel(
    feat, fidx, w, qkvw, ow, bias, norm_gain, attn_gain, out,
    featv, wb, qkv, outw, u, lhs, acc, hid, nbuf, kb0, kb1, kb2, kb3, qbuf, mbuf, lbuf, mix, obuf, rbuf,
    local_sem, y_send, y_recv, ring_send, ring_on, ring_recv, s_send, s_recv, h_send, h_recv,
    home_send, home_recv, col_send, col_recv, pair_send, pair_recv, ret_send, ret_recv,
):
    chans = feat.shape[-1]
    width = feat.shape[-2]
    t = lax.axis_index("tm")
    space = lax.axis_index("space")
    y = lax.axis_index("dp")
    z, x = lax.div(space, XS), lax.rem(space, XS)
    left, right, across = lax.rem(x + XS - 1, XS), lax.rem(x + 1, XS), lax.rem(x + 2, XS)
    down, up = lax.rem(z + ZS - 1, ZS), lax.rem(z + 1, ZS)
    before, after = lax.rem(space + XS * ZS - 1, XS * ZS), lax.rem(space + 1, XS * ZS)
    parity = lax.rem(z, 2)
    slot = lax.div(z, 2)
    same = t == parity

    def dev(core, row, col):
        return {"tm": core, "space": row * XS + col}

    sib, lft, rgt = dev(1 - t, z, x), dev(t, z, left), dev(t, z, right)
    dwn, upw = dev(t, down, x), dev(t, up, x)

    def rows(start, count):
        return pl.ds(pl.multiple_of(start, 16), count)

    mine = (
        pltpu.make_async_copy(w, wb.at[rows(y * QUARTER, QUARTER)], local_sem.at[0]),
        pltpu.make_async_copy(qkvw, qkv.at[rows(y * 96, 96)], local_sem.at[1]),
        pltpu.make_async_copy(ow, outw.at[rows(y * 96, 96)], local_sem.at[2]),
    )
    fetch = pltpu.make_async_copy(feat.at[0], featv, local_sem.at[3])
    fetch.start()
    barrier = pltpu.get_barrier_semaphore()

    def greet(device):
        pl.semaphore_signal(barrier, inc=1, device_id=device, device_id_type=MESH)

    for d in range(1, YS):
        greet({"dp": lax.rem(y + d, YS)})
    for device in (sib, lft, rgt):
        greet(device)
    for core in range(2):
        for d in range(1, ZS):
            greet(dev(core, lax.rem(z + d, ZS), x))
    greet({"space": before})
    greet({"space": after})
    for c in mine:
        c.start()
    fetch.wait()

    pad = jnp.zeros((WIDE - width, chans), F32)
    for f in range(3):
        for r in range(2):
            scaled = rms_scale(featv[f, r], norm_gain[...])
            act = scaled * jax.nn.sigmoid(scaled)
            u[1 + r, 2 + f] = jnp.concatenate([act, pad], axis=0).astype(BF)
    blank = jnp.zeros((3, WIDE, chans), BF)

    @pl.when(space == 0)
    def _():
        u[0, 2:5] = blank
        u[0, 0:2] = blank[:2]

    @pl.when(space == XS * ZS - 1)
    def _():
        u[3, 2:5] = blank
        u[3, 0:2] = blank[:2]

    @pl.when(t == 0)
    def _():
        for r in range(4):
            u[r, 0:2] = blank[:2]

    pl.semaphore_wait(barrier, YS - 1 + 3 + 2 * (ZS - 1) + 2)

    def copy(src, dst, send, rec, device):
        return pltpu.make_async_remote_copy(
            src_ref=src, dst_ref=dst, send_sem=send, recv_sem=rec, device_id=device, device_id_type=MESH
        )

    def landed(ref, sem):
        copy(ref, ref, s_send.at[0, 0], sem, sib).wait_recv()

    owner = [lax.rem(y + d, YS) for d in (3, 1, 2)]
    target = [{"dp": lax.rem(y + d, YS)} for d in (1, 3, 2)]

    def rim(src, dst, n, device):
        return copy(src, dst, h_send.at[n], h_recv.at[n], device)

    has_after, has_before = space < XS * ZS - 1, space > 0
    rims = (
        (has_after, rim(u.at[2, 2:5], u.at[0, 2:5], 0, {"space": after})),
        (has_before, rim(u.at[1, 2:5], u.at[3, 2:5], 1, {"space": before})),
    )
    prior = (
        (t == 0, rim(u.at[1:3, 3:5], u.at[1:3, 0:2], 2, sib)),
        (jnp.logical_and(t == 0, has_before), rim(u.at[0, 3:5], u.at[0, 0:2], 3, sib)),
        (jnp.logical_and(t == 0, has_after), rim(u.at[3, 3:5], u.at[3, 0:2], 4, sib)),
    )

    def send_rims():
        for cond, c in rims:
            pl.when(cond)(c.start)
        pl.when(t == 0)(prior[0][1].start)

    def take_rims():
        pl.when(has_before)(rims[0][1].wait_recv)
        pl.when(has_after)(rims[1][1].wait_recv)
        for cond, c in prior[1:]:
            pl.when(cond)(c.start)

    def take_prior():
        for cond, (_, c) in zip(
            (t == 1, jnp.logical_and(t == 1, has_before), jnp.logical_and(t == 1, has_after)), prior
        ):
            pl.when(cond)(c.wait_recv)

    keep = [[(fidx[0, f] >= 2 - kt).astype(F32) for f in range(3)] for kt in range(2)]

    def spread(g, r):
        cells = u[r, g].astype(F32)
        for kw in range(3):
            moved = cells if kw == 1 else pltpu.roll(cells, 1 if kw == 0 else WIDE - 1, 0)
            for kt in range(3):
                f = g - kt
                if 0 <= f < 3:
                    lhs[kt * 3 + kw, f, r] = (moved if kt == 2 else moved * keep[kt][f]).astype(BF)

    def spread_own():
        for g in range(2, 5):
            for r in range(1, 3):
                spread(g, r)

    def spread_rims():
        for g in range(2, 5):
            spread(g, 0)
            spread(g, 3)

    def spread_prior():
        for g in range(2):
            for r in range(4):
                spread(g, r)

    def tap(number):
        if isinstance(number, int):
            kt, kh, kw = number // 9, (number // 3) % 3, number % 3
        else:
            kt, kh, kw = lax.div(number, 9), lax.rem(lax.div(number, 3), 3), lax.rem(number, 3)
        cells = lhs[kt * 3 + kw, :, pl.ds(kh, 2)].reshape(-1, chans)
        acc[...] += dot(cells, wb[rows(number * chans, chans)])

    def taps(j, first, last):
        @pl.loop(first, last)
        def _(i):
            tap(7 * j + i)

    def half_rows(j, core):
        return rows(j * QUARTER + core * HALF, HALF)

    def rest_rows(j, core):
        return rows(j * QUARTER + 2 * HALF + core * REST, REST)

    def proj_rows(j, core):
        return rows(j * 96 + core * 48, 48)

    def small_refs(j, core):
        return wb.at[rest_rows(j, core)], qkv.at[proj_rows(j, core)], outw.at[proj_rows(j, core)]

    def ring_core(core):
        sent = []

        def go(c):
            c.start()
            sent.append(c)

        def push(ref, send, rec, device):
            go(copy(ref, ref, send, rec, device))

        def piece(j, n, part=0, parts=1):
            size = XPIECE if core == 0 else ZPIECE
            return wb.at[rows(j * QUARTER + core * HALF + n * size + part * (size // parts), size // parts)]

        place = x if core == 0 else z
        size = XPIECE if core == 0 else ZPIECE
        ahead, behind = (rgt, lft) if core == 0 else (upw, dwn)

        def to_y(k):
            src = w.at[rows(core * HALF + place * size, size)]
            go(copy(src, piece(y, place), y_send.at[k, 0], y_recv.at[k, 0], target[k]))

        def to_y_small(k):
            srcs = w.at[rows(2 * HALF + core * REST, REST)], qkvw.at[rows(core * 48, 48)], ow.at[rows(core * 48, 48)]
            for n, (src, dst) in enumerate(zip(srcs, small_refs(y, core))):
                go(copy(src, dst, y_send.at[k, 1 + n], y_recv.at[k, 1 + n], target[k]))

        def from_y(k):
            ref = piece(owner[k], place)
            landed(ref, y_recv.at[k, 0])
            push(ref, ring_send.at[k, 0], ring_recv.at[k, 0], ahead)
            push(ref, ring_send.at[k, 1], ring_recv.at[k, 1], behind)

        def small(k):
            for n, ref in enumerate(small_refs(owner[k], core)):
                landed(ref, y_recv.at[k, 1 + n])
                push(ref, s_send.at[k, 1 + n], s_recv.at[k, 1 + n], sib)

        count = XS if core == 0 else ZS
        last = count // 2

        def step(k, d):
            for way, on in enumerate((ahead, behind)):
                n = lax.rem(place + (count - d if way == 0 else d), count)
                landed(piece(owner[k], n), ring_recv.at[k, 2 * d - 2 + way])
                ref = piece(owner[k], n)
                if d == last - 1:
                    ref = piece(owner[k], n, way, 2)
                push(ref, ring_on.at[k, 2 * d - 2 + way], ring_recv.at[k, 2 * d + way], on)

        def end(k):
            n = lax.rem(place + last, count)
            for way in range(2):
                landed(piece(owner[k], n, way, 2), ring_recv.at[k, 2 * last - 2 + way])
            push(wb.at[half_rows(owner[k], core)], s_send.at[k, 0], s_recv.at[k, 0], sib)

        def shared(k):
            landed(wb.at[half_rows(owner[k], 1 - core)], s_recv.at[k, 0])
            landed(wb.at[rest_rows(owner[k], 1 - core)], s_recv.at[k, 1])

        to_y(0)
        to_y(1)
        send_rims()
        acc[...] = jnp.zeros_like(acc)
        spread_own()
        from_y(0)
        from_y(1)
        to_y(2)
        for k in range(3):
            to_y_small(k)
        take_rims()
        if core == 0:
            spread_rims()
            step(0, 1)
            step(1, 1)
            from_y(2)
            take_prior()
            spread_prior()
            end(0)
            end(1)
            step(2, 1)
            mine[0].wait()
            taps(y, 0, 4)
            end(2)
            taps(y, 4, 6)
            for k in range(3):
                small(k)
        else:
            step(0, 1)
            step(1, 1)
            spread_rims()
            from_y(2)
            step(0, 2)
            step(1, 2)
            take_prior()
            spread_prior()
            step(0, 3)
            step(1, 3)
            step(2, 1)
            mine[0].wait()
            taps(y, 0, 3)
            end(0)
            end(1)
            step(2, 2)
            for k in range(3):
                small(k)
            taps(y, 3, 6)
            step(2, 3)
        shared(0)
        if core == 0:
            taps(owner[0], 0, 6)
        else:
            taps(owner[0], 0, 4)
            end(2)
            taps(owner[0], 4, 6)
        shared(1)
        taps(owner[1], 0, 6)
        shared(2)
        taps(owner[2], 0, 6)
        for c in sent:
            c.wait_send()

    for core in range(2):
        @pl.when(t == core)
        def _():
            ring_core(core)

    for number in (6, 13, 20):
        tap(number)

    for f in range(3):
        both = []
        for r in range(2):
            part = acc[pl.ds((f * 2 + r) * WIDE, width)]
            both.append(featv[f, r].astype(F32) + part + bias[...])
        hid[f] = jnp.concatenate(both, axis=0).astype(BF)
        nbuf[f] = rms_scale(hid[f], attn_gain[...]).astype(BF)

    kbs = (kb0, kb1, kb2, kb3)

    def home_copy(c, j):
        first, count = CHUNKS[c]
        dst = kbs[c].at[x, parity, slot]
        return copy(
            nbuf.at[j, pl.ds(first, count)], dst, home_send.at[c, j], home_recv.at[c, slot], dev(parity, 2 * j + t, x)
        )

    for c in range(4):
        for j in range(3):
            pl.when(2 * j + t != z)(home_copy(c, j).start)

    for k in range(3):
        landed(qkv.at[proj_rows(owner[k], 1 - t)], s_recv.at[k, 2])
        landed(outw.at[proj_rows(owner[k], 1 - t)], s_recv.at[k, 3])
    mine[1].wait()
    mine[2].wait()

    is_worker = z < 6

    @pl.when(is_worker)
    def _():
        sent = []

        def push(ref, send, rec, device):
            c = copy(ref, ref, send, rec, device)
            c.start()
            sent.append(c)

        def own(c):
            first, count = CHUNKS[c]

            @pl.when(same)
            def _():
                kbs[c][x, t, slot] = nbuf[slot, pl.ds(first, count)]

            for h in range(4):
                @pl.when(jnp.logical_not(jnp.logical_and(same, slot == h)))
                def _():
                    landed(kbs[c].at[x, t, h], home_recv.at[c, h])

            ref = kbs[c].at[x, t]
            push(ref, col_send.at[c, 0], col_recv.at[c, 0], rgt)
            push(ref, col_send.at[c, 1], col_recv.at[c, 1], lft)
            push(ref, pair_send.at[c, 0], pair_recv.at[c, 0], sib)

        def beside(c):
            for way, (col, on) in enumerate(((left, rgt), (right, lft))):
                ref = kbs[c].at[col, t]
                landed(ref, col_recv.at[c, way])
                push(kbs[c].at[col, t, pl.ds(2 * way, 2)], col_send.at[c, 2 + way], col_recv.at[c, 2 + way], on)
                push(ref, pair_send.at[c, 1 + way], pair_recv.at[c, 1 + way], sib)

        def far(c):
            for way in range(2):
                landed(kbs[c].at[across, t, pl.ds(2 * way, 2)], col_recv.at[c, 2 + way])
            push(kbs[c].at[across, t], pair_send.at[c, 3], pair_recv.at[c, 3], sib)

        def others(c):
            for n, col in enumerate((x, left, right, across)):
                landed(kbs[c].at[col, 1 - t], pair_recv.at[c, n])

        def project(c):
            first, count = CHUNKS[c]
            n = kbs[c][x, t].reshape(-1, chans)
            q = dot(n, qkv[:, :chans]).astype(BF)
            qk = dot_t(q, qkv[:, chans : 2 * chans]) * (math.log2(math.e) / math.sqrt(chans))
            qbuf[:, pl.ds(first, count)] = qk.astype(BF).reshape(4, count, chans)

        def attend(i, c):
            keys = kbs[c][...].reshape(-1, chans)
            s = dot_t(qbuf[i], keys)
            top = jnp.max(s, axis=-1, keepdims=True)
            if c > 0:
                top = jnp.maximum(top, mbuf[i])
            p = jnp.exp2(s - top)
            total = jnp.sum(p, axis=-1, keepdims=True)
            mixed = dot(p.astype(BF), keys)
            if c > 0:
                alpha = jnp.exp2(mbuf[i] - top)
                total = total + lbuf[i] * alpha
                mixed = mixed + mix[i] * alpha
            mbuf[i] = top
            lbuf[i] = total
            mix[i] = mixed

        def back(i):
            return copy(obuf.at[i], rbuf.at[slot], ret_send.at[i], ret_recv.at[slot], dev(parity, 2 * i + t, x))

        def finish(i):
            mixed = (mix[i] * (1.0 / lbuf[i])).astype(BF)
            attended = dot(mixed, qkv[:, 2 * chans :]).astype(BF)
            at_home = jnp.logical_and(same, slot == i)

            @pl.when(at_home)
            def _():
                rbuf[slot] = attended

            @pl.when(jnp.logical_not(at_home))
            def _():
                obuf[i] = attended
                back(i).start()

        own(0)
        project(0)
        own(1)
        project(1)
        beside(0)
        own(2)
        project(2)
        beside(1)
        far(0)
        own(3)
        project(3)
        others(0)
        attend(0, 0)
        beside(2)
        attend(1, 0)
        far(1)
        attend(2, 0)
        attend(3, 0)
        others(1)
        attend(0, 1)
        beside(3)
        attend(1, 1)
        far(2)
        attend(2, 1)
        attend(3, 1)
        others(2)
        attend(0, 2)
        attend(1, 2)
        far(3)
        attend(2, 2)
        attend(3, 2)
        others(3)

        @pl.loop(0, 4)
        def _(n):
            i = lax.rem(slot + 2 + jnp.where(n == 1, 3, jnp.where(n == 2, 1, n * 2)), 4)
            attend(i, 3)
            finish(i)

        for c in sent:
            c.wait_send()
        for i in range(4):
            pl.when(jnp.logical_not(jnp.logical_and(same, slot == i)))(back(i).wait_send)

    for j in range(3):
        @pl.when(2 * j + t != z)
        def _():
            for c in range(4):
                home_copy(c, j).wait_send()
            landed(rbuf.at[j], ret_recv.at[j])

        result = hid[j].astype(F32) + dot(rbuf[j], outw[...])
        for r in range(2):
            out[0, j, r] = result[r * width : (r + 1) * width].astype(BF)

    for cond, c in rims + prior:
        pl.when(cond)(c.wait_send)


def on_device(
    features, frame_index, conv_weight, conv_bias, norm_gain, attn_gain, qkv_weight, out_weight
):
    frames, height, width, chans = features.shape[1:]
    pixels = height * width
    vmem = pl.BlockSpec(memory_space=pltpu.VMEM)
    smem = pl.BlockSpec(memory_space=pltpu.SMEM)
    hbm = pl.BlockSpec(memory_space=pltpu.HBM)
    dma = pltpu.SemaphoreType.DMA
    blocks = [pltpu.VMEM((XS, 2, 4, count, chans), BF) for _, count in CHUNKS]
    return pl.pallas_call(
        kernel,
        out_shape=jax.ShapeDtypeStruct(features.shape, BF),
        in_specs=[hbm, smem, hbm, hbm, hbm, vmem, vmem, vmem],
        out_specs=vmem,
        scratch_shapes=[
            pltpu.VMEM((frames, height, width, chans), BF),
            pltpu.VMEM((YS * QUARTER, chans), BF),
            pltpu.VMEM((chans, 3 * chans), BF),
            pltpu.VMEM((chans, chans), BF),
            pltpu.VMEM((4, 5, WIDE, chans), BF),
            pltpu.VMEM((9, 3, 4, WIDE, chans), BF),
            pltpu.VMEM((6 * WIDE, chans), F32),
            pltpu.VMEM((frames, pixels, chans), BF),
            pltpu.VMEM((frames, pixels, chans), BF),
            *blocks,
            pltpu.VMEM((4, pixels, chans), BF),
            pltpu.VMEM((4, pixels, 1), F32),
            pltpu.VMEM((4, pixels, 1), F32),
            pltpu.VMEM((4, pixels, chans), F32),
            pltpu.VMEM((4, pixels, chans), BF),
            pltpu.VMEM((3, pixels, chans), BF),
            dma((4,)), dma((3, 4)), dma((3, 4)), dma((3, 2)), dma((3, 6)), dma((3, 8)),
            dma((3, 4)), dma((3, 4)), dma((5,)), dma((5,)),
            dma((4, 3)), dma((4, 4)), dma((4, 4)), dma((4, 4)), dma((4, 4)), dma((4, 4)), dma((4,)), dma((3,)),
        ],
        compiler_params=pltpu.CompilerParams(
            collective_id=1, has_side_effects=True, vmem_limit_bytes=60 * 1024 * 1024
        ),
        cost_estimate=pl.CostEstimate(
            flops=2 * frames * pixels * chans * chans * 31 + 4 * 4 * pixels * 32 * pixels * chans,
            bytes_accessed=4 * frames * pixels * chans + 2 * QUARTER * chans,
            transcendentals=4 * pixels * 32 * pixels,
        ),
    )(features, frame_index, conv_weight, qkv_weight, out_weight, conv_bias, norm_gain, attn_gain)


def solution(mesh):
    placed = (
        P("dp", "tm", "space", None, None),
        P("dp", "tm"),
        P("dp", None),
        P(),
        P(),
        P(),
        P("dp", None),
        P("dp", None),
    )
    return jax.shard_map(
        on_device,
        mesh=mesh,
        in_specs=placed,
        out_specs=P("dp", "tm", "space", None, None),
        check_vma=False,
    )
```

```python
import math

import jax
import jax.numpy as jnp
from jax import lax
from jax.experimental import pallas as pl
from jax.experimental.pallas import tpu as pltpu
from jax.sharding import PartitionSpec as P

EPS = 1e-06
MESH = pl.DeviceIdType.MESH
BF = jnp.bfloat16
F32 = jnp.float32
XS = 4
ZS = 8
YS = 4
QUARTER = 2592
XPART = 1152
ZPART = 896
REST = 272
XPIECE = XPART // XS
ZPIECE = ZPART // ZS
WIDE = 112
CHUNKS = ((0, 48), (48, 48), (96, 48), (144, 64))


def rms_scale(values, gain):
    values = values.astype(F32)
    return values * lax.rsqrt(jnp.mean(values * values, axis=-1, keepdims=True) + EPS) * gain


def dot(a, b):
    return jnp.dot(a, b, preferred_element_type=F32)


def dot_t(a, b):
    return lax.dot_general(a, b, (((1,), (1,)), ((), ())), preferred_element_type=F32)


def kernel(
    feat, fidx, w, qkvw, ow, bias, norm_gain, attn_gain, out,
    featv, wb, qkv, outw, u, lhs, acc, hid, nbuf, kb0, kb1, kb2, kb3, q0, q1, m0, m1, l0, l1, mix0, mix1, obuf, rbuf,
    local_sem, y_send, y_recv, ring_send, ring_on, ring_recv, s_send, s_recv, p_send, p_recv, h_send, h_recv,
    home_send, home_recv, col_send, col_recv, pair_send, pair_recv, ret_send, ret_recv,
):
    chans = feat.shape[-1]
    width = feat.shape[-2]
    t = lax.axis_index("tm")
    space = lax.axis_index("space")
    y = lax.axis_index("dp")
    z, x = lax.div(space, XS), lax.rem(space, XS)
    left, right, across = lax.rem(x + XS - 1, XS), lax.rem(x + 1, XS), lax.rem(x + 2, XS)
    down, up = lax.rem(z + ZS - 1, ZS), lax.rem(z + 1, ZS)
    before, after = lax.rem(space + XS * ZS - 1, XS * ZS), lax.rem(space + 1, XS * ZS)
    parity = lax.rem(z, 2)
    slot = lax.div(z, 2)
    same = t == parity

    def dev(core, row, col):
        return {"tm": core, "space": row * XS + col}

    sib, lft, rgt = dev(1 - t, z, x), dev(t, z, left), dev(t, z, right)
    dwn, upw = dev(t, down, x), dev(t, up, x)
    dwn2, upw2 = dev(t, lax.rem(z + ZS - 2, ZS), x), dev(t, lax.rem(z + 2, ZS), x)

    def rows(start, count):
        return pl.ds(pl.multiple_of(start, 16), count)

    mine = (
        pltpu.make_async_copy(w, wb.at[rows(y * QUARTER, QUARTER)], local_sem.at[0]),
        pltpu.make_async_copy(qkvw, qkv.at[rows(y * 96, 96)], local_sem.at[1]),
        pltpu.make_async_copy(ow, outw.at[rows(y * 96, 96)], local_sem.at[2]),
    )
    fetch = pltpu.make_async_copy(feat.at[0], featv, local_sem.at[3])
    fetch.start()
    barrier = pltpu.get_barrier_semaphore()

    def greet(device):
        pl.semaphore_signal(barrier, inc=1, device_id=device, device_id_type=MESH)

    for d in range(1, YS):
        greet({"dp": lax.rem(y + d, YS)})
    for device in (sib, lft, rgt):
        greet(device)
    for core in range(2):
        for d in range(1, ZS):
            greet(dev(core, lax.rem(z + d, ZS), x))
    greet({"space": before})
    greet({"space": after})
    for c in mine:
        c.start()

    blank = jnp.zeros((3, WIDE, chans), BF)

    @pl.when(space == 0)
    def _():
        u[0, 2:5] = blank
        u[0, 0:2] = blank[:2]

    @pl.when(space == XS * ZS - 1)
    def _():
        u[3, 2:5] = blank
        u[3, 0:2] = blank[:2]

    @pl.when(t == 0)
    def _():
        for r in range(4):
            u[r, 0:2] = blank[:2]

    pl.semaphore_wait(barrier, YS - 1 + 3 + 2 * (ZS - 1) + 2)

    def activate():
        fetch.wait()
        pad = jnp.zeros((WIDE - width, chans), F32)
        for f in range(3):
            for r in range(2):
                scaled = rms_scale(featv[f, r], norm_gain[...])
                act = scaled * jax.nn.sigmoid(scaled)
                u[1 + r, 2 + f] = jnp.concatenate([act, pad], axis=0).astype(BF)

    def copy(src, dst, send, rec, device):
        return pltpu.make_async_remote_copy(
            src_ref=src, dst_ref=dst, send_sem=send, recv_sem=rec, device_id=device, device_id_type=MESH
        )

    def landed(ref, sem):
        copy(ref, ref, s_send.at[0, 0], sem, sib).wait_recv()

    owner = [lax.rem(y + d, YS) for d in (3, 1, 2)]
    target = [{"dp": lax.rem(y + d, YS)} for d in (1, 3, 2)]

    def rim(src, dst, n, device):
        return copy(src, dst, h_send.at[n], h_recv.at[n], device)

    has_after, has_before = space < XS * ZS - 1, space > 0
    rims = (
        (has_after, rim(u.at[2, 2:5], u.at[0, 2:5], 0, {"space": after})),
        (has_before, rim(u.at[1, 2:5], u.at[3, 2:5], 1, {"space": before})),
    )
    prior = (
        (t == 0, rim(u.at[1:3, 3:5], u.at[1:3, 0:2], 2, sib)),
        (jnp.logical_and(t == 0, has_before), rim(u.at[0, 3:5], u.at[0, 0:2], 3, sib)),
        (jnp.logical_and(t == 0, has_after), rim(u.at[3, 3:5], u.at[3, 0:2], 4, sib)),
    )

    def send_rims():
        for cond, c in rims:
            pl.when(cond)(c.start)
        pl.when(t == 0)(prior[0][1].start)

    def take_rims():
        pl.when(has_before)(rims[0][1].wait_recv)
        pl.when(has_after)(rims[1][1].wait_recv)
        for cond, c in prior[1:]:
            pl.when(cond)(c.start)

    def take_prior():
        for cond, (_, c) in zip(
            (t == 1, jnp.logical_and(t == 1, has_before), jnp.logical_and(t == 1, has_after)), prior
        ):
            pl.when(cond)(c.wait_recv)

    keep = [[(fidx[0, f] >= 2 - kt).astype(F32) for f in range(3)] for kt in range(2)]

    def spread(g, r):
        cells = u[r, g].astype(F32)
        for kw in range(3):
            moved = cells if kw == 1 else pltpu.roll(cells, 1 if kw == 0 else WIDE - 1, 0)
            for kt in range(3):
                f = g - kt
                if 0 <= f < 3:
                    lhs[kt * 3 + kw, f, r] = (moved if kt == 2 else moved * keep[kt][f]).astype(BF)

    def spread_own():
        for g in range(2, 5):
            for r in range(1, 3):
                spread(g, r)

    def spread_rims():
        for g in range(2, 5):
            spread(g, 0)
            spread(g, 3)

    def spread_prior():
        for g in range(2):
            for r in range(4):
                spread(g, r)

    def window(number):
        if isinstance(number, int):
            kt, kh, kw = number // 9, (number // 3) % 3, number % 3
        else:
            kt, kh, kw = lax.div(number, 9), lax.rem(lax.div(number, 3), 3), lax.rem(number, 3)
        return lhs[kt * 3 + kw, :, pl.ds(kh, 2)].reshape(-1, chans)

    def three_taps(j, half):
        first = 7 * j + 3 * half
        cells = jnp.concatenate([window(first + n) for n in range(3)], axis=1)
        acc[...] += dot(cells, wb[rows(first * chans, 3 * chans)])

    def six_taps(j):
        three_taps(j, 0)
        three_taps(j, 1)

    def rest_rows(j, core):
        return rows(j * QUARTER + XPART + ZPART + core * REST, REST)

    sent = [], []

    def small_refs(j, core):
        part = rows(j * 96 + core * 48, 48)
        return qkv.at[part], outw.at[part]

    def small_copies(k):
        part = rows(t * 48, 48)
        return [
            copy(src, dst, y_send.at[k, 2 + n], y_recv.at[k, 2 + n], target[k])
            for n, (src, dst) in enumerate(zip((qkvw.at[part], ow.at[part]), small_refs(y, t)))
        ]

    def small_shares(k):
        return [copy(ref, ref, p_send.at[k, n], p_recv.at[k, n], sib) for n, ref in enumerate(small_refs(owner[k], t))]

    def ring_core(core):
        def go(src, dst, count, send, rec, device):
            copy(src, dst, send[0].at[send[1], send[2]], rec, device).start()
            sent[core].append((count, send))

        size = XPIECE if core == 0 else ZPIECE
        place = x if core == 0 else z

        def piece(j, n, part=0, parts=1):
            start = j * QUARTER + core * XPART + n * size + part * (size // parts)
            return wb.at[rows(start, size // parts)]

        def to_y(k):
            src = w.at[rows(core * XPART + place * size, size)]
            go(src, piece(y, place), size, (y_send, k, 0), y_recv.at[k, 0], target[k])

        def to_y_rest(k):
            src = w.at[rows(XPART + ZPART + core * REST, REST)]
            go(src, wb.at[rest_rows(y, core)], REST, (y_send, k, 1), y_recv.at[k, 1], target[k])

        def push(ref, send, rec, device, count=size):
            go(ref, ref, count, send, rec, device)

        def share(k, n, ref):
            push(ref, (s_send, k, n), s_recv.at[k, n], sib)

        def rest(k):
            ref = wb.at[rest_rows(owner[k], core)]
            landed(ref, y_recv.at[k, 1])
            push(ref, (s_send, k, 8), s_recv.at[k, 8], sib, REST)

        def from_y(k):
            ref = piece(owner[k], place)
            landed(ref, y_recv.at[k, 0])
            for n, on in enumerate((rgt, lft) if core == 0 else (upw, dwn, upw2, dwn2)):
                push(ref, (ring_send, k, n), ring_recv.at[k, n], on)
            share(k, 0, ref)

        def x_on(k):
            for way, (n, on) in enumerate(((left, rgt), (right, lft))):
                ref = piece(owner[k], n)
                landed(ref, ring_recv.at[k, way])
                half = piece(owner[k], n, way, 2)
                push(half, (ring_on, k, way), ring_recv.at[k, 2 + way], on, size // 2)
                share(k, 1 + way, ref)

        def z_on(k):
            for way, far in enumerate((ZS - 1, 1)):
                ref = piece(owner[k], lax.rem(z + far, ZS))
                landed(ref, ring_recv.at[k, way])
                share(k, 1 + way, ref)
            for way, (far, one, two) in enumerate(((ZS - 2, upw, upw2), (2, dwn, dwn2))):
                ref = piece(owner[k], lax.rem(z + far, ZS))
                landed(ref, ring_recv.at[k, 2 + way])
                push(ref, (ring_on, k, way), ring_recv.at[k, 4 + way], one)
                if way == k % 2:
                    push(ref, (ring_on, k, 2), ring_recv.at[k, 6], two)
                share(k, 3 + way, ref)

        def end(k):
            if core == 0:
                for way in range(2):
                    landed(piece(owner[k], across, way, 2), ring_recv.at[k, 2 + way])
                share(k, 3, piece(owner[k], across))
            else:
                for n, far in ((4, ZS - 3), (5, 3), (6, 4)):
                    ref = piece(owner[k], lax.rem(z + far, ZS))
                    landed(ref, ring_recv.at[k, n])
                    share(k, n + 1, ref)

        def shared(k):
            start = owner[k] * QUARTER
            if core == 0:
                for n, far in enumerate((0, ZS - 1, 1, ZS - 2, 2, ZS - 3, 3, 4)):
                    first = start + XPART + lax.rem(z + far, ZS) * ZPIECE
                    landed(wb.at[rows(first, ZPIECE)], s_recv.at[k, n])
            else:
                for n, col in enumerate((x, left, right, across)):
                    landed(wb.at[rows(start + col * XPIECE, XPIECE)], s_recv.at[k, n])
            landed(wb.at[rest_rows(owner[k], 1 - core)], s_recv.at[k, 8])

        on = x_on if core == 0 else z_on
        for k in range(3):
            to_y(k)
        for k in range(3):
            to_y_rest(k)
        for k in range(3):
            for c in small_copies(k):
                c.start()
        activate()
        send_rims()
        acc[...] = jnp.zeros_like(acc)
        spread_own()
        for k in range(3):
            from_y(k)
        on(0)
        take_rims()
        spread_rims()
        on(1)
        take_prior()
        spread_prior()
        on(2)
        mine[0].wait()
        end(0)
        three_taps(y, 0)
        rest(0)
        end(1)
        rest(1)
        end(2)
        rest(2)
        three_taps(y, 1)
        for k in range(3):
            shared(k)
            six_taps(owner[k])

    for core in range(2):
        @pl.when(t == core)
        def _():
            ring_core(core)

    acc[...] += sum(dot(window(n), wb[rows(n * chans, chans)]) for n in (6, 13, 20))

    for f in range(3):
        both = []
        for r in range(2):
            part = acc[pl.ds((f * 2 + r) * WIDE, width)]
            both.append(featv[f, r].astype(F32) + part + bias[...])
        hid[f] = jnp.concatenate(both, axis=0).astype(BF)
        nbuf[f] = rms_scale(hid[f], attn_gain[...]).astype(BF)

    kbs = (kb0, kb1, kb2, kb3)
    groups = (q0, m0, l0, mix0), (q1, m1, l1, mix1)

    def home_copy(c, j):
        first, count = CHUNKS[c]
        dst = kbs[c].at[x, parity, slot]
        return copy(
            nbuf.at[j, pl.ds(first, count)], dst, home_send.at[c, j], home_recv.at[c, slot], dev(parity, 2 * j + t, x)
        )

    for c in range(4):
        for j in range(3):
            pl.when(2 * j + t != z)(home_copy(c, j).start)

    for k in range(3):
        for n, ref in enumerate(small_refs(owner[k], t)):
            landed(ref, y_recv.at[k, 2 + n])
        for c in small_shares(k):
            c.start()
    for k in range(3):
        for n, ref in enumerate(small_refs(owner[k], 1 - t)):
            landed(ref, p_recv.at[k, n])
    mine[1].wait()
    mine[2].wait()

    is_worker = z < 6

    @pl.when(is_worker)
    def _():
        sent = []

        def push(ref, send, rec, device):
            c = copy(ref, ref, send, rec, device)
            c.start()
            sent.append(c)

        def own(c):
            first, count = CHUNKS[c]

            @pl.when(same)
            def _():
                kbs[c][x, t, slot] = nbuf[slot, pl.ds(first, count)]

            for h in range(4):
                @pl.when(jnp.logical_not(jnp.logical_and(same, slot == h)))
                def _():
                    landed(kbs[c].at[x, t, h], home_recv.at[c, h])

            ref = kbs[c].at[x, t]
            push(ref, col_send.at[c, 0], col_recv.at[c, 0], rgt)
            push(ref, col_send.at[c, 1], col_recv.at[c, 1], lft)
            push(ref, pair_send.at[c, 0], pair_recv.at[c, 0], sib)

        def beside(c):
            for way, (col, on) in enumerate(((left, rgt), (right, lft))):
                ref = kbs[c].at[col, t]
                landed(ref, col_recv.at[c, way])
                push(kbs[c].at[col, t, pl.ds(2 * way, 2)], col_send.at[c, 2 + way], col_recv.at[c, 2 + way], on)
                push(ref, pair_send.at[c, 1 + way], pair_recv.at[c, 1 + way], sib)

        def far(c):
            for way in range(2):
                landed(kbs[c].at[across, t, pl.ds(2 * way, 2)], col_recv.at[c, 2 + way])
            push(kbs[c].at[across, t], pair_send.at[c, 3], pair_recv.at[c, 3], sib)

        def others(c):
            for n, col in enumerate((x, left, right, across)):
                landed(kbs[c].at[col, 1 - t], pair_recv.at[c, n])

        def project(c):
            count = CHUNKS[c][1]
            n = kbs[c][x, t].reshape(-1, chans)
            q = dot(n, qkv[:, :chans]).astype(BF)
            qk = dot_t(q, qkv[:, chans : 2 * chans]) * (math.log2(math.e) / math.sqrt(chans))
            groups[c // 2][0][pl.ds(0 if c % 2 == 0 else 4 * CHUNKS[c - 1][1], 4 * count)] = qk.astype(BF)

        def attend(group, c):
            queries, maxima, sums, mix = groups[group]
            keys = kbs[c][...].reshape(-1, chans)
            s = dot_t(queries[...], keys)
            top = jnp.max(s, axis=-1, keepdims=True)
            if c > 0:
                top = jnp.maximum(top, maxima[...])
            p = jnp.exp2(s - top)
            total = jnp.sum(p, axis=-1, keepdims=True)
            mixed = dot(p.astype(BF), keys)
            if c > 0:
                alpha = jnp.exp2(maxima[...] - top)
                total = total + sums[...] * alpha
                mixed = mixed + mix[...] * alpha
            maxima[...] = top
            sums[...] = total
            mix[...] = mixed

        def back(group, i):
            first, count = CHUNKS[2 * group][0], CHUNKS[2 * group][1] + CHUNKS[2 * group + 1][1]
            part = pl.ds(first, count)
            return copy(
                obuf.at[i, part], rbuf.at[slot, part], ret_send.at[group, i], ret_recv.at[slot, group],
                dev(parity, 2 * i + t, x),
            )

        def finish(group):
            _, _, sums, mix = groups[group]
            mixed = (mix[...] * (1.0 / sums[...])).astype(BF)
            attended = dot(mixed, qkv[:, 2 * chans :]).astype(BF)
            start = 0
            for c in (2 * group, 2 * group + 1):
                first, count = CHUNKS[c]
                for i in range(4):
                    obuf[i, pl.ds(first, count)] = attended[start : start + count]
                    start += count
            for n in range(4):
                i = lax.rem(slot + (2, 1, 3, 0)[n], 4)

                @pl.when(jnp.logical_not(jnp.logical_and(same, slot == i)))
                def _():
                    back(group, i).start()

        own(0)
        project(0)
        own(1)
        project(1)
        beside(0)
        own(2)
        beside(1)
        far(0)
        project(2)
        others(0)
        attend(0, 0)
        own(3)
        project(3)
        beside(2)
        far(1)
        attend(1, 0)
        others(1)
        beside(3)
        attend(0, 1)
        far(2)
        attend(1, 1)
        others(2)
        attend(0, 2)
        attend(1, 2)
        far(3)
        others(3)
        for group in range(2):
            attend(group, 3)
            finish(group)

        @pl.when(same)
        def _():
            rbuf[slot] = obuf[slot]

        for c in sent:
            c.wait_send()
        for i in range(4):
            @pl.when(jnp.logical_not(jnp.logical_and(same, slot == i)))
            def _():
                for group in range(2):
                    back(group, i).wait_send()

    for j in range(3):
        @pl.when(2 * j + t != z)
        def _():
            for c in range(4):
                home_copy(c, j).wait_send()
            for group in range(2):
                part = pl.ds(CHUNKS[2 * group][0], CHUNKS[2 * group][1] + CHUNKS[2 * group + 1][1])
                landed(rbuf.at[j, part], ret_recv.at[j, group])

        result = hid[j].astype(F32) + dot(rbuf[j], outw[...])
        for r in range(2):
            out[0, j, r] = result[r * width : (r + 1) * width].astype(BF)

    for cond, c in rims + prior:
        pl.when(cond)(c.wait_send)
    for k in range(3):
        for c in small_copies(k) + small_shares(k):
            c.wait_send()
    for core in range(2):
        @pl.when(t == core)
        def _():
            for count, (sems, k, n) in sent[core]:
                ref = wb.at[pl.ds(0, count)]
                copy(ref, ref, sems.at[k, n], s_recv.at[0, 0], sib).wait_send()


def on_device(
    features, frame_index, conv_weight, conv_bias, norm_gain, attn_gain, qkv_weight, out_weight
):
    frames, height, width, chans = features.shape[1:]
    pixels = height * width
    vmem = pl.BlockSpec(memory_space=pltpu.VMEM)
    smem = pl.BlockSpec(memory_space=pltpu.SMEM)
    hbm = pl.BlockSpec(memory_space=pltpu.HBM)
    dma = pltpu.SemaphoreType.DMA
    queries = [4 * (CHUNKS[c][1] + CHUNKS[c + 1][1]) for c in (0, 2)]
    blocks = [pltpu.VMEM((XS, 2, 4, count, chans), BF) for _, count in CHUNKS]
    return pl.pallas_call(
        kernel,
        out_shape=jax.ShapeDtypeStruct(features.shape, BF),
        in_specs=[hbm, smem, hbm, hbm, hbm, vmem, vmem, vmem],
        out_specs=vmem,
        scratch_shapes=[
            pltpu.VMEM((frames, height, width, chans), BF),
            pltpu.VMEM((YS * QUARTER, chans), BF),
            pltpu.VMEM((chans, 3 * chans), BF),
            pltpu.VMEM((chans, chans), BF),
            pltpu.VMEM((4, 5, WIDE, chans), BF),
            pltpu.VMEM((9, 3, 4, WIDE, chans), BF),
            pltpu.VMEM((6 * WIDE, chans), F32),
            pltpu.VMEM((frames, pixels, chans), BF),
            pltpu.VMEM((frames, pixels, chans), BF),
            *blocks,
            *[pltpu.VMEM((n, chans), BF) for n in queries],
            *[pltpu.VMEM((n, 1), F32) for n in queries * 2],
            *[pltpu.VMEM((n, chans), F32) for n in queries],
            pltpu.VMEM((4, pixels, chans), BF),
            pltpu.VMEM((3, pixels, chans), BF),
            dma((4,)), dma((3, 4)), dma((3, 4)), dma((3, 4)), dma((3, 3)), dma((3, 7)),
            dma((3, 9)), dma((3, 9)), dma((3, 2)), dma((3, 2)), dma((5,)), dma((5,)),
            dma((4, 3)), dma((4, 4)), dma((4, 4)), dma((4, 4)), dma((4, 4)), dma((4, 4)), dma((2, 4)), dma((3, 2)),
        ],
        compiler_params=pltpu.CompilerParams(
            collective_id=1, has_side_effects=True, vmem_limit_bytes=60 * 1024 * 1024
        ),
        cost_estimate=pl.CostEstimate(
            flops=2 * frames * pixels * chans * chans * 31 + 4 * 4 * pixels * 32 * pixels * chans,
            bytes_accessed=4 * frames * pixels * chans + 2 * QUARTER * chans,
            transcendentals=4 * pixels * 32 * pixels,
        ),
    )(features, frame_index, conv_weight, qkv_weight, out_weight, conv_bias, norm_gain, attn_gain)


def solution(mesh):
    placed = (
        P("dp", "tm", "space", None, None),
        P("dp", "tm"),
        P("dp", None),
        P(),
        P(),
        P(),
        P("dp", None),
        P("dp", None),
    )
    return jax.shard_map(
        on_device,
        mesh=mesh,
        in_specs=placed,
        out_specs=P("dp", "tm", "space", None, None),
        check_vma=False,
    )
```

```python
import math

import jax
import jax.numpy as jnp
from jax import lax
from jax.experimental import pallas as pl
from jax.experimental.pallas import tpu as pltpu
from jax.sharding import PartitionSpec as P

EPS = 1e-06
MESH = pl.DeviceIdType.MESH
BF = jnp.bfloat16
F32 = jnp.float32
XS = 4
ZS = 8
YS = 4
QUARTER = 2592
XPART = 1152
ZPART = 896
REST = 272
XPIECE = XPART // XS
ZPIECE = ZPART // ZS
WIDE = 112
CHUNKS = ((0, 48), (48, 48), (96, 48), (144, 64))


def rms_scale(values, gain):
    values = values.astype(F32)
    return values * lax.rsqrt(jnp.mean(values * values, axis=-1, keepdims=True) + EPS) * gain


def dot(a, b):
    return jnp.dot(a, b, preferred_element_type=F32)


def dot_t(a, b):
    return lax.dot_general(a, b, (((1,), (1,)), ((), ())), preferred_element_type=F32)


def kernel(
    feat, fidx, w, qkvw, ow, bias, norm_gain, attn_gain, out,
    featv, wb, qkv, outw, u, lhs, acc, hid, nbuf, kb0, kb1, kb2, kb3, q0, q1, m0, m1, l0, l1, mix0, mix1, obuf, rbuf,
    local_sem, y_send, y_recv, ring_send, ring_on, ring_recv, s_send, s_recv, p_send, p_recv, h_send, h_recv,
    home_send, home_recv, col_send, col_recv, pair_send, pair_recv, ret_send, ret_recv,
):
    chans = feat.shape[-1]
    width = feat.shape[-2]
    t = lax.axis_index("tm")
    space = lax.axis_index("space")
    y = lax.axis_index("dp")
    z, x = lax.div(space, XS), lax.rem(space, XS)
    left, right, across = lax.rem(x + XS - 1, XS), lax.rem(x + 1, XS), lax.rem(x + 2, XS)
    down, up = lax.rem(z + ZS - 1, ZS), lax.rem(z + 1, ZS)
    before, after = lax.rem(space + XS * ZS - 1, XS * ZS), lax.rem(space + 1, XS * ZS)
    parity = lax.rem(z, 2)
    slot = lax.div(z, 2)
    same = t == parity

    def dev(core, row, col):
        return {"tm": core, "space": row * XS + col}

    sib, lft, rgt = dev(1 - t, z, x), dev(t, z, left), dev(t, z, right)
    dwn, upw = dev(t, down, x), dev(t, up, x)
    dwn2, upw2 = dev(t, lax.rem(z + ZS - 2, ZS), x), dev(t, lax.rem(z + 2, ZS), x)

    def rows(start, count):
        return pl.ds(pl.multiple_of(start, 16), count)

    mine = (
        pltpu.make_async_copy(w, wb.at[rows(y * QUARTER, QUARTER)], local_sem.at[0]),
        pltpu.make_async_copy(qkvw, qkv.at[rows(y * 96, 96)], local_sem.at[1]),
        pltpu.make_async_copy(ow, outw.at[rows(y * 96, 96)], local_sem.at[2]),
    )
    fetch = pltpu.make_async_copy(feat.at[0], featv, local_sem.at[3])
    fetch.start()
    barrier = pltpu.get_barrier_semaphore()

    def greet(device):
        pl.semaphore_signal(barrier, inc=1, device_id=device, device_id_type=MESH)

    for d in range(1, YS):
        greet({"dp": lax.rem(y + d, YS)})
    for device in (sib, lft, rgt):
        greet(device)
    for core in range(2):
        for d in range(1, ZS):
            greet(dev(core, lax.rem(z + d, ZS), x))
    greet({"space": before})
    greet({"space": after})
    for c in mine:
        c.start()

    blank = jnp.zeros((3, WIDE, chans), BF)

    @pl.when(space == 0)
    def _():
        u[0, 2:5] = blank
        u[0, 0:2] = blank[:2]

    @pl.when(space == XS * ZS - 1)
    def _():
        u[3, 2:5] = blank
        u[3, 0:2] = blank[:2]

    @pl.when(t == 0)
    def _():
        for r in range(4):
            u[r, 0:2] = blank[:2]

    pl.semaphore_wait(barrier, YS - 1 + 3 + 2 * (ZS - 1) + 2)

    def activate():
        fetch.wait()
        pad = jnp.zeros((WIDE - width, chans), F32)
        for f in range(3):
            for r in range(2):
                scaled = rms_scale(featv[f, r], norm_gain[...])
                act = scaled * jax.nn.sigmoid(scaled)
                u[1 + r, 2 + f] = jnp.concatenate([act, pad], axis=0).astype(BF)

    def copy(src, dst, send, rec, device):
        return pltpu.make_async_remote_copy(
            src_ref=src, dst_ref=dst, send_sem=send, recv_sem=rec, device_id=device, device_id_type=MESH
        )

    def landed(ref, sem):
        copy(ref, ref, s_send.at[0, 0], sem, sib).wait_recv()

    owner = [lax.rem(y + d, YS) for d in (3, 1, 2)]
    target = [{"dp": lax.rem(y + d, YS)} for d in (1, 3, 2)]

    def rim(src, dst, n, device):
        return copy(src, dst, h_send.at[n], h_recv.at[n], device)

    has_after, has_before = space < XS * ZS - 1, space > 0
    rims = (
        (has_after, rim(u.at[2, 2:5], u.at[0, 2:5], 0, {"space": after})),
        (has_before, rim(u.at[1, 2:5], u.at[3, 2:5], 1, {"space": before})),
    )
    prior = (
        (t == 0, rim(u.at[1:3, 3:5], u.at[1:3, 0:2], 2, sib)),
        (jnp.logical_and(t == 0, has_before), rim(u.at[0, 3:5], u.at[0, 0:2], 3, sib)),
        (jnp.logical_and(t == 0, has_after), rim(u.at[3, 3:5], u.at[3, 0:2], 4, sib)),
    )

    def send_rims():
        for cond, c in rims:
            pl.when(cond)(c.start)
        pl.when(t == 0)(prior[0][1].start)

    def take_rims():
        pl.when(has_before)(rims[0][1].wait_recv)
        pl.when(has_after)(rims[1][1].wait_recv)
        for cond, c in prior[1:]:
            pl.when(cond)(c.start)

    def take_prior():
        for cond, (_, c) in zip(
            (t == 1, jnp.logical_and(t == 1, has_before), jnp.logical_and(t == 1, has_after)), prior
        ):
            pl.when(cond)(c.wait_recv)

    keep = [[(fidx[0, f] >= 2 - kt).astype(F32) for f in range(3)] for kt in range(2)]

    def spread(g, r):
        cells = u[r, g].astype(F32)
        for kw in range(3):
            moved = cells if kw == 1 else pltpu.roll(cells, 1 if kw == 0 else WIDE - 1, 0)
            for kt in range(3):
                f = g - kt
                if 0 <= f < 3:
                    lhs[kt * 3 + kw, f, r] = (moved if kt == 2 else moved * keep[kt][f]).astype(BF)

    def spread_own():
        for g in range(2, 5):
            for r in range(1, 3):
                spread(g, r)

    def spread_rims():
        for g in range(2, 5):
            spread(g, 0)
            spread(g, 3)

    def spread_prior():
        for g in range(2):
            for r in range(4):
                spread(g, r)

    def window(number):
        if isinstance(number, int):
            kt, kh, kw = number // 9, (number // 3) % 3, number % 3
        else:
            kt, kh, kw = lax.div(number, 9), lax.rem(lax.div(number, 3), 3), lax.rem(number, 3)
        return lhs[kt * 3 + kw, :, pl.ds(kh, 2)].reshape(-1, chans)

    def three_taps(j, half):
        first = 7 * j + 3 * half
        cells = jnp.concatenate([window(first + n) for n in range(3)], axis=1)
        acc[...] += dot(cells, wb[rows(first * chans, 3 * chans)])

    def six_taps(j):
        three_taps(j, 0)
        three_taps(j, 1)

    def rest_rows(j, core):
        return rows(j * QUARTER + XPART + ZPART + core * REST, REST)

    sent = [], []

    def small_refs(j, core):
        part = rows(j * 96 + core * 48, 48)
        return qkv.at[part], outw.at[part]

    def small_copies(k):
        part = rows(t * 48, 48)
        return [
            copy(src, dst, y_send.at[k, 2 + n], y_recv.at[k, 2 + n], target[k])
            for n, (src, dst) in enumerate(zip((qkvw.at[part], ow.at[part]), small_refs(y, t)))
        ]

    def small_shares(k):
        return [copy(ref, ref, p_send.at[k, n], p_recv.at[k, n], sib) for n, ref in enumerate(small_refs(owner[k], t))]

    def ring_core(core):
        def go(src, dst, count, send, rec, device):
            copy(src, dst, send[0].at[send[1], send[2]], rec, device).start()
            sent[core].append((count, send))

        size = XPIECE if core == 0 else ZPIECE
        place = x if core == 0 else z

        def piece(j, n, part=0, parts=1):
            start = j * QUARTER + core * XPART + n * size + part * (size // parts)
            return wb.at[rows(start, size // parts)]

        def to_y(k):
            src = w.at[rows(core * XPART + place * size, size)]
            go(src, piece(y, place), size, (y_send, k, 0), y_recv.at[k, 0], target[k])

        def to_y_rest(k):
            src = w.at[rows(XPART + ZPART + core * REST, REST)]
            go(src, wb.at[rest_rows(y, core)], REST, (y_send, k, 1), y_recv.at[k, 1], target[k])

        def push(ref, send, rec, device, count=size):
            go(ref, ref, count, send, rec, device)

        def share(k, n, ref):
            push(ref, (s_send, k, n), s_recv.at[k, n], sib)

        def rest(k):
            ref = wb.at[rest_rows(owner[k], core)]
            landed(ref, y_recv.at[k, 1])
            push(ref, (s_send, k, 8), s_recv.at[k, 8], sib, REST)

        def from_y(k):
            ref = piece(owner[k], place)
            landed(ref, y_recv.at[k, 0])
            for n, on in enumerate((rgt, lft) if core == 0 else (upw, dwn, upw2, dwn2)):
                push(ref, (ring_send, k, n), ring_recv.at[k, n], on)
            share(k, 0, ref)

        def x_on(k):
            for way, (n, on) in enumerate(((left, rgt), (right, lft))):
                ref = piece(owner[k], n)
                landed(ref, ring_recv.at[k, way])
                half = piece(owner[k], n, way, 2)
                push(half, (ring_on, k, way), ring_recv.at[k, 2 + way], on, size // 2)
                share(k, 1 + way, ref)

        def z_on(k):
            for way, far in enumerate((ZS - 1, 1)):
                ref = piece(owner[k], lax.rem(z + far, ZS))
                landed(ref, ring_recv.at[k, way])
                share(k, 1 + way, ref)
            for way, (far, one, two) in enumerate(((ZS - 2, upw, upw2), (2, dwn, dwn2))):
                ref = piece(owner[k], lax.rem(z + far, ZS))
                landed(ref, ring_recv.at[k, 2 + way])
                push(ref, (ring_on, k, way), ring_recv.at[k, 4 + way], one)
                if way == k % 2:
                    push(ref, (ring_on, k, 2), ring_recv.at[k, 6], two)
                share(k, 3 + way, ref)

        def end(k):
            if core == 0:
                for way in range(2):
                    landed(piece(owner[k], across, way, 2), ring_recv.at[k, 2 + way])
                share(k, 3, piece(owner[k], across))
            else:
                for n, far in ((4, ZS - 3), (5, 3), (6, 4)):
                    ref = piece(owner[k], lax.rem(z + far, ZS))
                    landed(ref, ring_recv.at[k, n])
                    share(k, n + 1, ref)

        def shared(k):
            start = owner[k] * QUARTER
            if core == 0:
                for n, far in enumerate((0, ZS - 1, 1, ZS - 2, 2, ZS - 3, 3, 4)):
                    first = start + XPART + lax.rem(z + far, ZS) * ZPIECE
                    landed(wb.at[rows(first, ZPIECE)], s_recv.at[k, n])
            else:
                for n, col in enumerate((x, left, right, across)):
                    landed(wb.at[rows(start + col * XPIECE, XPIECE)], s_recv.at[k, n])
            landed(wb.at[rest_rows(owner[k], 1 - core)], s_recv.at[k, 8])

        on = x_on if core == 0 else z_on
        for k in range(3):
            to_y(k)
        for k in range(3):
            to_y_rest(k)
        for k in range(3):
            for c in small_copies(k):
                c.start()
        activate()
        send_rims()
        acc[...] = jnp.zeros_like(acc)
        spread_own()
        for k in range(3):
            from_y(k)
        on(0)
        take_rims()
        spread_rims()
        on(1)
        take_prior()
        spread_prior()
        on(2)
        mine[0].wait()
        three_taps(y, 0)
        end(0)
        rest(0)
        three_taps(y, 1)
        end(1)
        rest(1)
        shared(0)
        three_taps(owner[0], 0)
        end(2)
        rest(2)
        three_taps(owner[0], 1)
        shared(1)
        six_taps(owner[1])
        shared(2)
        six_taps(owner[2])

    for core in range(2):
        @pl.when(t == core)
        def _():
            ring_core(core)

    acc[...] += sum(dot(window(n), wb[rows(n * chans, chans)]) for n in (6, 13, 20))

    for f in range(3):
        both = []
        for r in range(2):
            part = acc[pl.ds((f * 2 + r) * WIDE, width)]
            both.append(featv[f, r].astype(F32) + part + bias[...])
        hid[f] = jnp.concatenate(both, axis=0).astype(BF)
        nbuf[f] = rms_scale(hid[f], attn_gain[...]).astype(BF)

    kbs = (kb0, kb1, kb2, kb3)
    groups = (q0, m0, l0, mix0), (q1, m1, l1, mix1)

    def home_copy(c, j):
        first, count = CHUNKS[c]
        dst = kbs[c].at[x, parity, slot]
        return copy(
            nbuf.at[j, pl.ds(first, count)], dst, home_send.at[c, j], home_recv.at[c, slot], dev(parity, 2 * j + t, x)
        )

    for c in range(4):
        for j in range(3):
            pl.when(2 * j + t != z)(home_copy(c, j).start)

    for k in range(3):
        for n, ref in enumerate(small_refs(owner[k], t)):
            landed(ref, y_recv.at[k, 2 + n])
        for c in small_shares(k):
            c.start()
    for k in range(3):
        for n, ref in enumerate(small_refs(owner[k], 1 - t)):
            landed(ref, p_recv.at[k, n])
    mine[1].wait()
    mine[2].wait()

    is_worker = z < 6

    @pl.when(is_worker)
    def _():
        sent = []

        def push(ref, send, rec, device):
            c = copy(ref, ref, send, rec, device)
            c.start()
            sent.append(c)

        def own(c):
            first, count = CHUNKS[c]

            @pl.when(same)
            def _():
                kbs[c][x, t, slot] = nbuf[slot, pl.ds(first, count)]

            for h in range(4):
                @pl.when(jnp.logical_not(jnp.logical_and(same, slot == h)))
                def _():
                    landed(kbs[c].at[x, t, h], home_recv.at[c, h])

            ref = kbs[c].at[x, t]
            push(ref, col_send.at[c, 0], col_recv.at[c, 0], rgt)
            push(ref, col_send.at[c, 1], col_recv.at[c, 1], lft)
            push(ref, pair_send.at[c, 0], pair_recv.at[c, 0], sib)

        def beside(c):
            for way, (col, on) in enumerate(((left, rgt), (right, lft))):
                ref = kbs[c].at[col, t]
                landed(ref, col_recv.at[c, way])
                push(kbs[c].at[col, t, pl.ds(2 * way, 2)], col_send.at[c, 2 + way], col_recv.at[c, 2 + way], on)
                push(ref, pair_send.at[c, 1 + way], pair_recv.at[c, 1 + way], sib)

        def far(c):
            for way in range(2):
                landed(kbs[c].at[across, t, pl.ds(2 * way, 2)], col_recv.at[c, 2 + way])
            push(kbs[c].at[across, t], pair_send.at[c, 3], pair_recv.at[c, 3], sib)

        def others(c):
            for n, col in enumerate((x, left, right, across)):
                landed(kbs[c].at[col, 1 - t], pair_recv.at[c, n])

        def project(c):
            count = CHUNKS[c][1]
            n = kbs[c][x, t].reshape(-1, chans)
            q = dot(n, qkv[:, :chans]).astype(BF)
            qk = dot_t(q, qkv[:, chans : 2 * chans]) * (math.log2(math.e) / math.sqrt(chans))
            groups[c // 2][0][pl.ds(0 if c % 2 == 0 else 4 * CHUNKS[c - 1][1], 4 * count)] = qk.astype(BF)

        def attend(group, c):
            queries, maxima, sums, mix = groups[group]
            keys = kbs[c][...].reshape(-1, chans)
            s = dot_t(queries[...], keys)
            top = jnp.max(s, axis=-1, keepdims=True)
            if c > 0:
                top = jnp.maximum(top, maxima[...])
            p = jnp.exp2(s - top)
            total = jnp.sum(p, axis=-1, keepdims=True)
            mixed = dot(p.astype(BF), keys)
            if c > 0:
                alpha = jnp.exp2(maxima[...] - top)
                total = total + sums[...] * alpha
                mixed = mixed + mix[...] * alpha
            maxima[...] = top
            sums[...] = total
            mix[...] = mixed

        def back(group, i):
            first, count = CHUNKS[2 * group][0], CHUNKS[2 * group][1] + CHUNKS[2 * group + 1][1]
            part = pl.ds(first, count)
            return copy(
                obuf.at[i, part], rbuf.at[slot, part], ret_send.at[group, i], ret_recv.at[slot, group],
                dev(parity, 2 * i + t, x),
            )

        def finish(group):
            _, _, sums, mix = groups[group]
            mixed = (mix[...] * (1.0 / sums[...])).astype(BF)
            attended = dot(mixed, qkv[:, 2 * chans :]).astype(BF)
            start = 0
            for c in (2 * group, 2 * group + 1):
                first, count = CHUNKS[c]
                for i in range(4):
                    obuf[i, pl.ds(first, count)] = attended[start : start + count]
                    start += count
            for n in range(4):
                i = lax.rem(slot + (2, 1, 3, 0)[n], 4)

                @pl.when(jnp.logical_not(jnp.logical_and(same, slot == i)))
                def _():
                    back(group, i).start()

        own(0)
        project(0)
        own(1)
        project(1)
        beside(0)
        own(2)
        project(2)
        beside(1)
        far(0)
        own(3)
        project(3)
        others(0)
        attend(0, 0)
        beside(2)
        far(1)
        attend(1, 0)
        beside(3)
        others(1)
        attend(0, 1)
        far(2)
        attend(1, 1)
        others(2)
        attend(0, 2)
        far(3)
        attend(1, 2)
        others(3)
        for group in range(2):
            attend(group, 3)
            finish(group)

        @pl.when(same)
        def _():
            rbuf[slot] = obuf[slot]

        for c in sent:
            c.wait_send()
        for i in range(4):
            @pl.when(jnp.logical_not(jnp.logical_and(same, slot == i)))
            def _():
                for group in range(2):
                    back(group, i).wait_send()

    for j in range(3):
        @pl.when(2 * j + t != z)
        def _():
            for c in range(4):
                home_copy(c, j).wait_send()
            for group in range(2):
                part = pl.ds(CHUNKS[2 * group][0], CHUNKS[2 * group][1] + CHUNKS[2 * group + 1][1])
                landed(rbuf.at[j, part], ret_recv.at[j, group])

        result = hid[j].astype(F32) + dot(rbuf[j], outw[...])
        for r in range(2):
            out[0, j, r] = result[r * width : (r + 1) * width].astype(BF)

    for cond, c in rims + prior:
        pl.when(cond)(c.wait_send)
    for k in range(3):
        for c in small_copies(k) + small_shares(k):
            c.wait_send()
    for core in range(2):
        @pl.when(t == core)
        def _():
            for count, (sems, k, n) in sent[core]:
                ref = wb.at[pl.ds(0, count)]
                copy(ref, ref, sems.at[k, n], s_recv.at[0, 0], sib).wait_send()


def on_device(
    features, frame_index, conv_weight, conv_bias, norm_gain, attn_gain, qkv_weight, out_weight
):
    frames, height, width, chans = features.shape[1:]
    pixels = height * width
    vmem = pl.BlockSpec(memory_space=pltpu.VMEM)
    smem = pl.BlockSpec(memory_space=pltpu.SMEM)
    hbm = pl.BlockSpec(memory_space=pltpu.HBM)
    dma = pltpu.SemaphoreType.DMA
    queries = [4 * (CHUNKS[c][1] + CHUNKS[c + 1][1]) for c in (0, 2)]
    blocks = [pltpu.VMEM((XS, 2, 4, count, chans), BF) for _, count in CHUNKS]
    return pl.pallas_call(
        kernel,
        out_shape=jax.ShapeDtypeStruct(features.shape, BF),
        in_specs=[hbm, smem, hbm, hbm, hbm, vmem, vmem, vmem],
        out_specs=vmem,
        scratch_shapes=[
            pltpu.VMEM((frames, height, width, chans), BF),
            pltpu.VMEM((YS * QUARTER, chans), BF),
            pltpu.VMEM((chans, 3 * chans), BF),
            pltpu.VMEM((chans, chans), BF),
            pltpu.VMEM((4, 5, WIDE, chans), BF),
            pltpu.VMEM((9, 3, 4, WIDE, chans), BF),
            pltpu.VMEM((6 * WIDE, chans), F32),
            pltpu.VMEM((frames, pixels, chans), BF),
            pltpu.VMEM((frames, pixels, chans), BF),
            *blocks,
            *[pltpu.VMEM((n, chans), BF) for n in queries],
            *[pltpu.VMEM((n, 1), F32) for n in queries * 2],
            *[pltpu.VMEM((n, chans), F32) for n in queries],
            pltpu.VMEM((4, pixels, chans), BF),
            pltpu.VMEM((3, pixels, chans), BF),
            dma((4,)), dma((3, 4)), dma((3, 4)), dma((3, 4)), dma((3, 3)), dma((3, 7)),
            dma((3, 9)), dma((3, 9)), dma((3, 2)), dma((3, 2)), dma((5,)), dma((5,)),
            dma((4, 3)), dma((4, 4)), dma((4, 4)), dma((4, 4)), dma((4, 4)), dma((4, 4)), dma((2, 4)), dma((3, 2)),
        ],
        compiler_params=pltpu.CompilerParams(
            collective_id=1, has_side_effects=True, vmem_limit_bytes=60 * 1024 * 1024
        ),
        cost_estimate=pl.CostEstimate(
            flops=2 * frames * pixels * chans * chans * 31 + 4 * 4 * pixels * 32 * pixels * chans,
            bytes_accessed=4 * frames * pixels * chans + 2 * QUARTER * chans,
            transcendentals=4 * pixels * 32 * pixels,
        ),
    )(features, frame_index, conv_weight, qkv_weight, out_weight, conv_bias, norm_gain, attn_gain)


def solution(mesh):
    placed = (
        P("dp", "tm", "space", None, None),
        P("dp", "tm"),
        P("dp", None),
        P(),
        P(),
        P(),
        P("dp", None),
        P("dp", None),
    )
    return jax.shard_map(
        on_device,
        mesh=mesh,
        in_specs=placed,
        out_specs=P("dp", "tm", "space", None, None),
        check_vma=False,
    )
```

```python
import math

import jax
import jax.numpy as jnp
from jax import lax
from jax.experimental import pallas as pl
from jax.experimental.pallas import tpu as pltpu
from jax.sharding import PartitionSpec as P

EPS = 1e-06
MESH = pl.DeviceIdType.MESH
BF = jnp.bfloat16
F32 = jnp.float32
XS = 4
ZS = 8
YS = 4
QUARTER = 2592
XPART = 1152
ZPART = 896
REST = 272
XPIECE = XPART // XS
ZPIECE = ZPART // ZS
WIDE = 112
CHUNKS = ((0, 48), (48, 48), (96, 48), (144, 64))


def rms_scale(values, gain):
    values = values.astype(F32)
    return values * lax.rsqrt(jnp.mean(values * values, axis=-1, keepdims=True) + EPS) * gain


def dot(a, b):
    return jnp.dot(a, b, preferred_element_type=F32)


def dot_t(a, b):
    return lax.dot_general(a, b, (((1,), (1,)), ((), ())), preferred_element_type=F32)


def kernel(
    feat, fidx, w, qkvw, ow, bias, norm_gain, attn_gain, out,
    featv, wb, qkv, outw, u, lhs, acc, hid, nbuf, kb0, kb1, kb2, kb3, q0, q1, m0, m1, l0, l1, mix0, mix1, obuf, rbuf,
    local_sem, y_send, y_recv, ring_send, ring_on, ring_recv, s_send, s_recv, p_send, p_recv, h_send, h_recv,
    home_send, home_recv, col_send, col_recv, pair_send, pair_recv, ret_send, ret_recv,
):
    chans = feat.shape[-1]
    width = feat.shape[-2]
    t = lax.axis_index("tm")
    space = lax.axis_index("space")
    y = lax.axis_index("dp")
    z, x = lax.div(space, XS), lax.rem(space, XS)
    left, right, across = lax.rem(x + XS - 1, XS), lax.rem(x + 1, XS), lax.rem(x + 2, XS)
    down, up = lax.rem(z + ZS - 1, ZS), lax.rem(z + 1, ZS)
    before, after = lax.rem(space + XS * ZS - 1, XS * ZS), lax.rem(space + 1, XS * ZS)
    parity = lax.rem(z, 2)
    slot = lax.div(z, 2)
    same = t == parity

    def dev(core, row, col):
        return {"tm": core, "space": row * XS + col}

    sib, lft, rgt = dev(1 - t, z, x), dev(t, z, left), dev(t, z, right)
    dwn, upw = dev(t, down, x), dev(t, up, x)
    dwn2, upw2 = dev(t, lax.rem(z + ZS - 2, ZS), x), dev(t, lax.rem(z + 2, ZS), x)

    def rows(start, count):
        return pl.ds(pl.multiple_of(start, 16), count)

    mine = (
        pltpu.make_async_copy(w, wb.at[rows(y * QUARTER, QUARTER)], local_sem.at[0]),
        pltpu.make_async_copy(qkvw, qkv.at[rows(y * 96, 96)], local_sem.at[1]),
        pltpu.make_async_copy(ow, outw.at[rows(y * 96, 96)], local_sem.at[2]),
    )
    fetch = pltpu.make_async_copy(feat.at[0], featv, local_sem.at[3])
    fetch.start()
    barrier = pltpu.get_barrier_semaphore()

    def greet(device):
        pl.semaphore_signal(barrier, inc=1, device_id=device, device_id_type=MESH)

    for d in range(1, YS):
        greet({"dp": lax.rem(y + d, YS)})
    for device in (sib, lft, rgt):
        greet(device)
    for core in range(2):
        for d in range(1, ZS):
            greet(dev(core, lax.rem(z + d, ZS), x))
    greet({"space": before})
    greet({"space": after})
    for c in mine:
        c.start()

    blank = jnp.zeros((3, WIDE, chans), BF)

    @pl.when(space == 0)
    def _():
        u[0, 2:5] = blank
        u[0, 0:2] = blank[:2]

    @pl.when(space == XS * ZS - 1)
    def _():
        u[3, 2:5] = blank
        u[3, 0:2] = blank[:2]

    @pl.when(t == 0)
    def _():
        for r in range(4):
            u[r, 0:2] = blank[:2]

    pl.semaphore_wait(barrier, YS - 1 + 3 + 2 * (ZS - 1) + 2)

    def activate():
        fetch.wait()
        pad = jnp.zeros((WIDE - width, chans), F32)
        for f in range(3):
            for r in range(2):
                scaled = rms_scale(featv[f, r], norm_gain[...])
                act = scaled * jax.nn.sigmoid(scaled)
                u[1 + r, 2 + f] = jnp.concatenate([act, pad], axis=0).astype(BF)

    def copy(src, dst, send, rec, device):
        return pltpu.make_async_remote_copy(
            src_ref=src, dst_ref=dst, send_sem=send, recv_sem=rec, device_id=device, device_id_type=MESH
        )

    def landed(ref, sem):
        copy(ref, ref, s_send.at[0, 0], sem, sib).wait_recv()

    owner = [lax.rem(y + d, YS) for d in (3, 1, 2)]
    target = [{"dp": lax.rem(y + d, YS)} for d in (1, 3, 2)]

    def rim(src, dst, n, device):
        return copy(src, dst, h_send.at[n], h_recv.at[n], device)

    has_after, has_before = space < XS * ZS - 1, space > 0
    rims = (
        (has_after, rim(u.at[2, 2:5], u.at[0, 2:5], 0, {"space": after})),
        (has_before, rim(u.at[1, 2:5], u.at[3, 2:5], 1, {"space": before})),
    )
    prior = (
        (t == 0, rim(u.at[1:3, 3:5], u.at[1:3, 0:2], 2, sib)),
        (jnp.logical_and(t == 0, has_before), rim(u.at[0, 3:5], u.at[0, 0:2], 3, sib)),
        (jnp.logical_and(t == 0, has_after), rim(u.at[3, 3:5], u.at[3, 0:2], 4, sib)),
    )

    def send_rims():
        for cond, c in rims:
            pl.when(cond)(c.start)
        pl.when(t == 0)(prior[0][1].start)

    def take_rims():
        pl.when(has_before)(rims[0][1].wait_recv)
        pl.when(has_after)(rims[1][1].wait_recv)
        for cond, c in prior[1:]:
            pl.when(cond)(c.start)

    def take_prior():
        for cond, (_, c) in zip(
            (t == 1, jnp.logical_and(t == 1, has_before), jnp.logical_and(t == 1, has_after)), prior
        ):
            pl.when(cond)(c.wait_recv)

    keep = [[(fidx[0, f] >= 2 - kt).astype(F32) for f in range(3)] for kt in range(2)]

    def spread(g, r):
        cells = u[r, g].astype(F32)
        for kw in range(3):
            moved = cells if kw == 1 else pltpu.roll(cells, 1 if kw == 0 else WIDE - 1, 0)
            for kt in range(3):
                f = g - kt
                if 0 <= f < 3:
                    lhs[kt * 3 + kw, f, r] = (moved if kt == 2 else moved * keep[kt][f]).astype(BF)

    def spread_own():
        for g in range(2, 5):
            for r in range(1, 3):
                spread(g, r)

    def spread_rims():
        for g in range(2, 5):
            spread(g, 0)
            spread(g, 3)

    def spread_prior():
        for g in range(2):
            for r in range(4):
                spread(g, r)

    def window(number):
        if isinstance(number, int):
            kt, kh, kw = number // 9, (number // 3) % 3, number % 3
        else:
            kt, kh, kw = lax.div(number, 9), lax.rem(lax.div(number, 3), 3), lax.rem(number, 3)
        return lhs[kt * 3 + kw, :, pl.ds(kh, 2)].reshape(-1, chans)

    def three_taps(j, half):
        first = 7 * j + 3 * half
        cells = jnp.concatenate([window(first + n) for n in range(3)], axis=1)
        acc[...] += dot(cells, wb[rows(first * chans, 3 * chans)])

    def six_taps(j):
        three_taps(j, 0)
        three_taps(j, 1)

    def rest_rows(j, core):
        return rows(j * QUARTER + XPART + ZPART + core * REST, REST)

    sent = [], []

    def small_refs(j, core):
        part = rows(j * 96 + core * 48, 48)
        return qkv.at[part], outw.at[part]

    def small_copies(k):
        part = rows(t * 48, 48)
        return [
            copy(src, dst, y_send.at[k, 2 + n], y_recv.at[k, 2 + n], target[k])
            for n, (src, dst) in enumerate(zip((qkvw.at[part], ow.at[part]), small_refs(y, t)))
        ]

    def small_shares(k):
        return [copy(ref, ref, p_send.at[k, n], p_recv.at[k, n], sib) for n, ref in enumerate(small_refs(owner[k], t))]

    def ring_core(core):
        def go(src, dst, count, send, rec, device):
            copy(src, dst, send[0].at[send[1], send[2]], rec, device).start()
            sent[core].append((count, send))

        size = XPIECE if core == 0 else ZPIECE
        place = x if core == 0 else z

        def piece(j, n, part=0, parts=1):
            start = j * QUARTER + core * XPART + n * size + part * (size // parts)
            return wb.at[rows(start, size // parts)]

        def to_y(k):
            src = w.at[rows(core * XPART + place * size, size)]
            go(src, piece(y, place), size, (y_send, k, 0), y_recv.at[k, 0], target[k])

        def to_y_rest(k):
            src = w.at[rows(XPART + ZPART + core * REST, REST)]
            go(src, wb.at[rest_rows(y, core)], REST, (y_send, k, 1), y_recv.at[k, 1], target[k])

        def push(ref, send, rec, device, count=size):
            go(ref, ref, count, send, rec, device)

        def share(k, n, ref):
            push(ref, (s_send, k, n), s_recv.at[k, n], sib)

        def rest(k):
            ref = wb.at[rest_rows(owner[k], core)]
            landed(ref, y_recv.at[k, 1])
            push(ref, (s_send, k, 8), s_recv.at[k, 8], sib, REST)

        def from_y(k):
            ref = piece(owner[k], place)
            landed(ref, y_recv.at[k, 0])
            for n, on in enumerate((rgt, lft) if core == 0 else (upw, dwn, upw2, dwn2)):
                push(ref, (ring_send, k, n), ring_recv.at[k, n], on)
            share(k, 0, ref)

        def x_on(k):
            for way, (n, on) in enumerate(((left, rgt), (right, lft))):
                ref = piece(owner[k], n)
                landed(ref, ring_recv.at[k, way])
                half = piece(owner[k], n, way, 2)
                push(half, (ring_on, k, way), ring_recv.at[k, 2 + way], on, size // 2)
                share(k, 1 + way, ref)

        def z_on(k):
            for way, far in enumerate((ZS - 1, 1)):
                ref = piece(owner[k], lax.rem(z + far, ZS))
                landed(ref, ring_recv.at[k, way])
                share(k, 1 + way, ref)
            for way, (far, one, two) in enumerate(((ZS - 2, upw, upw2), (2, dwn, dwn2))):
                ref = piece(owner[k], lax.rem(z + far, ZS))
                landed(ref, ring_recv.at[k, 2 + way])
                push(ref, (ring_on, k, way), ring_recv.at[k, 4 + way], one)
                if way == k % 2:
                    push(ref, (ring_on, k, 2), ring_recv.at[k, 6], two)
                share(k, 3 + way, ref)

        def end(k):
            if core == 0:
                for way in range(2):
                    landed(piece(owner[k], across, way, 2), ring_recv.at[k, 2 + way])
                share(k, 3, piece(owner[k], across))
            else:
                for n, far in ((4, ZS - 3), (5, 3), (6, 4)):
                    ref = piece(owner[k], lax.rem(z + far, ZS))
                    landed(ref, ring_recv.at[k, n])
                    share(k, n + 1, ref)

        def shared(k):
            start = owner[k] * QUARTER
            if core == 0:
                for n, far in enumerate((0, ZS - 1, 1, ZS - 2, 2, ZS - 3, 3, 4)):
                    first = start + XPART + lax.rem(z + far, ZS) * ZPIECE
                    landed(wb.at[rows(first, ZPIECE)], s_recv.at[k, n])
            else:
                for n, col in enumerate((x, left, right, across)):
                    landed(wb.at[rows(start + col * XPIECE, XPIECE)], s_recv.at[k, n])
            landed(wb.at[rest_rows(owner[k], 1 - core)], s_recv.at[k, 8])

        on = x_on if core == 0 else z_on
        for k in range(3):
            to_y(k)
        for k in range(3):
            to_y_rest(k)
        for k in range(3):
            for c in small_copies(k):
                c.start()
        activate()
        send_rims()
        acc[...] = jnp.zeros_like(acc)
        spread_own()
        for k in range(3):
            from_y(k)
        on(0)
        take_rims()
        spread_rims()
        on(1)
        take_prior()
        spread_prior()
        mine[0].wait()
        three_taps(y, 0)
        on(2)
        end(0)
        rest(0)
        three_taps(y, 1)
        end(1)
        rest(1)
        shared(0)
        three_taps(owner[0], 0)
        end(2)
        rest(2)
        three_taps(owner[0], 1)
        shared(1)
        six_taps(owner[1])
        shared(2)
        six_taps(owner[2])

    for core in range(2):
        @pl.when(t == core)
        def _():
            ring_core(core)

    acc[...] += sum(dot(window(n), wb[rows(n * chans, chans)]) for n in (6, 13, 20))

    kbs = (kb0, kb1, kb2, kb3)
    groups = (q0, m0, l0, mix0), (q1, m1, l1, mix1)

    def home_copy(c, j):
        first, count = CHUNKS[c]
        dst = kbs[c].at[x, parity, slot]
        return copy(
            nbuf.at[j, pl.ds(first, count)], dst, home_send.at[c, j], home_recv.at[c, slot], dev(parity, 2 * j + t, x)
        )

    for f in range(3):
        both = []
        for r in range(2):
            part = acc[pl.ds((f * 2 + r) * WIDE, width)]
            both.append(featv[f, r].astype(F32) + part + bias[...])
        hid[f] = jnp.concatenate(both, axis=0).astype(BF)
        nbuf[f] = rms_scale(hid[f], attn_gain[...]).astype(BF)
        pl.when(2 * f + t != z)(home_copy(0, f).start)

    for c in range(1, 4):
        for j in range(3):
            pl.when(2 * j + t != z)(home_copy(c, j).start)

    for k in range(3):
        for n, ref in enumerate(small_refs(owner[k], t)):
            landed(ref, y_recv.at[k, 2 + n])
        for c in small_shares(k):
            c.start()
    for k in range(3):
        for n, ref in enumerate(small_refs(owner[k], 1 - t)):
            landed(ref, p_recv.at[k, n])
    mine[1].wait()
    mine[2].wait()

    is_worker = z < 6

    @pl.when(is_worker)
    def _():
        sent = []

        def push(ref, send, rec, device):
            c = copy(ref, ref, send, rec, device)
            c.start()
            sent.append(c)

        def own(c):
            first, count = CHUNKS[c]

            @pl.when(same)
            def _():
                kbs[c][x, t, slot] = nbuf[slot, pl.ds(first, count)]

            for h in range(4):
                @pl.when(jnp.logical_not(jnp.logical_and(same, slot == h)))
                def _():
                    landed(kbs[c].at[x, t, h], home_recv.at[c, h])

            ref = kbs[c].at[x, t]
            push(ref, col_send.at[c, 0], col_recv.at[c, 0], rgt)
            push(ref, col_send.at[c, 1], col_recv.at[c, 1], lft)
            push(ref, pair_send.at[c, 0], pair_recv.at[c, 0], sib)

        def beside(c):
            for way, (col, on) in enumerate(((left, rgt), (right, lft))):
                ref = kbs[c].at[col, t]
                landed(ref, col_recv.at[c, way])
                push(kbs[c].at[col, t, pl.ds(2 * way, 2)], col_send.at[c, 2 + way], col_recv.at[c, 2 + way], on)
                push(ref, pair_send.at[c, 1 + way], pair_recv.at[c, 1 + way], sib)

        def far(c):
            for way in range(2):
                landed(kbs[c].at[across, t, pl.ds(2 * way, 2)], col_recv.at[c, 2 + way])
            push(kbs[c].at[across, t], pair_send.at[c, 3], pair_recv.at[c, 3], sib)

        def others(c):
            for n, col in enumerate((x, left, right, across)):
                landed(kbs[c].at[col, 1 - t], pair_recv.at[c, n])

        def project(c):
            count = CHUNKS[c][1]
            n = kbs[c][x, t].reshape(-1, chans)
            q = dot(n, qkv[:, :chans]).astype(BF)
            qk = dot_t(q, qkv[:, chans : 2 * chans]) * (math.log2(math.e) / math.sqrt(chans))
            groups[c // 2][0][pl.ds(0 if c % 2 == 0 else 4 * CHUNKS[c - 1][1], 4 * count)] = qk.astype(BF)

        def attend(group, c):
            queries, maxima, sums, mix = groups[group]
            keys = kbs[c][...].reshape(-1, chans)
            s = dot_t(queries[...], keys)
            top = jnp.max(s, axis=-1, keepdims=True)
            if c > 0:
                top = jnp.maximum(top, maxima[...])
            p = jnp.exp2(s - top)
            total = jnp.sum(p, axis=-1, keepdims=True)
            mixed = dot(p.astype(BF), keys)
            if c > 0:
                alpha = jnp.exp2(maxima[...] - top)
                total = total + sums[...] * alpha
                mixed = mixed + mix[...] * alpha
            maxima[...] = top
            sums[...] = total
            mix[...] = mixed

        def back(group, i):
            first, count = CHUNKS[2 * group][0], CHUNKS[2 * group][1] + CHUNKS[2 * group + 1][1]
            part = pl.ds(first, count)
            return copy(
                obuf.at[i, part], rbuf.at[slot, part], ret_send.at[group, i], ret_recv.at[slot, group],
                dev(parity, 2 * i + t, x),
            )

        def finish(group):
            _, _, sums, mix = groups[group]
            mixed = (mix[...] * (1.0 / sums[...])).astype(BF)
            attended = dot(mixed, qkv[:, 2 * chans :]).astype(BF)
            start = 0
            for c in (2 * group, 2 * group + 1):
                first, count = CHUNKS[c]
                for i in range(4):
                    obuf[i, pl.ds(first, count)] = attended[start : start + count]
                    start += count
            for n in range(4):
                i = lax.rem(slot + (2, 1, 3, 0)[n], 4)

                @pl.when(jnp.logical_not(jnp.logical_and(same, slot == i)))
                def _():
                    back(group, i).start()

        own(0)
        project(0)
        own(1)
        project(1)
        beside(0)
        own(2)
        project(2)
        beside(1)
        far(0)
        own(3)
        project(3)
        others(0)
        attend(0, 0)
        beside(2)
        far(1)
        attend(1, 0)
        beside(3)
        others(1)
        attend(0, 1)
        far(2)
        attend(1, 1)
        others(2)
        attend(0, 2)
        far(3)
        attend(1, 2)
        others(3)
        for group in range(2):
            attend(group, 3)
            finish(group)

        @pl.when(same)
        def _():
            rbuf[slot] = obuf[slot]

        for c in sent:
            c.wait_send()
        for i in range(4):
            @pl.when(jnp.logical_not(jnp.logical_and(same, slot == i)))
            def _():
                for group in range(2):
                    back(group, i).wait_send()

    for j in range(3):
        @pl.when(2 * j + t != z)
        def _():
            for c in range(4):
                home_copy(c, j).wait_send()
            for group in range(2):
                part = pl.ds(CHUNKS[2 * group][0], CHUNKS[2 * group][1] + CHUNKS[2 * group + 1][1])
                landed(rbuf.at[j, part], ret_recv.at[j, group])

        result = hid[j].astype(F32) + dot(rbuf[j], outw[...])
        for r in range(2):
            out[0, j, r] = result[r * width : (r + 1) * width].astype(BF)

    for cond, c in rims + prior:
        pl.when(cond)(c.wait_send)
    for k in range(3):
        for c in small_copies(k) + small_shares(k):
            c.wait_send()
    for core in range(2):
        @pl.when(t == core)
        def _():
            for count, (sems, k, n) in sent[core]:
                ref = wb.at[pl.ds(0, count)]
                copy(ref, ref, sems.at[k, n], s_recv.at[0, 0], sib).wait_send()


def on_device(
    features, frame_index, conv_weight, conv_bias, norm_gain, attn_gain, qkv_weight, out_weight
):
    frames, height, width, chans = features.shape[1:]
    pixels = height * width
    vmem = pl.BlockSpec(memory_space=pltpu.VMEM)
    smem = pl.BlockSpec(memory_space=pltpu.SMEM)
    hbm = pl.BlockSpec(memory_space=pltpu.HBM)
    dma = pltpu.SemaphoreType.DMA
    queries = [4 * (CHUNKS[c][1] + CHUNKS[c + 1][1]) for c in (0, 2)]
    blocks = [pltpu.VMEM((XS, 2, 4, count, chans), BF) for _, count in CHUNKS]
    return pl.pallas_call(
        kernel,
        out_shape=jax.ShapeDtypeStruct(features.shape, BF),
        in_specs=[hbm, smem, hbm, hbm, hbm, vmem, vmem, vmem],
        out_specs=vmem,
        scratch_shapes=[
            pltpu.VMEM((frames, height, width, chans), BF),
            pltpu.VMEM((YS * QUARTER, chans), BF),
            pltpu.VMEM((chans, 3 * chans), BF),
            pltpu.VMEM((chans, chans), BF),
            pltpu.VMEM((4, 5, WIDE, chans), BF),
            pltpu.VMEM((9, 3, 4, WIDE, chans), BF),
            pltpu.VMEM((6 * WIDE, chans), F32),
            pltpu.VMEM((frames, pixels, chans), BF),
            pltpu.VMEM((frames, pixels, chans), BF),
            *blocks,
            *[pltpu.VMEM((n, chans), BF) for n in queries],
            *[pltpu.VMEM((n, 1), F32) for n in queries * 2],
            *[pltpu.VMEM((n, chans), F32) for n in queries],
            pltpu.VMEM((4, pixels, chans), BF),
            pltpu.VMEM((3, pixels, chans), BF),
            dma((4,)), dma((3, 4)), dma((3, 4)), dma((3, 4)), dma((3, 3)), dma((3, 7)),
            dma((3, 9)), dma((3, 9)), dma((3, 2)), dma((3, 2)), dma((5,)), dma((5,)),
            dma((4, 3)), dma((4, 4)), dma((4, 4)), dma((4, 4)), dma((4, 4)), dma((4, 4)), dma((2, 4)), dma((3, 2)),
        ],
        compiler_params=pltpu.CompilerParams(
            collective_id=1, has_side_effects=True, vmem_limit_bytes=60 * 1024 * 1024
        ),
        cost_estimate=pl.CostEstimate(
            flops=2 * frames * pixels * chans * chans * 31 + 4 * 4 * pixels * 32 * pixels * chans,
            bytes_accessed=4 * frames * pixels * chans + 2 * QUARTER * chans,
            transcendentals=4 * pixels * 32 * pixels,
        ),
    )(features, frame_index, conv_weight, qkv_weight, out_weight, conv_bias, norm_gain, attn_gain)


def solution(mesh):
    placed = (
        P("dp", "tm", "space", None, None),
        P("dp", "tm"),
        P("dp", None),
        P(),
        P(),
        P(),
        P("dp", None),
        P("dp", None),
    )
    return jax.shard_map(
        on_device,
        mesh=mesh,
        in_specs=placed,
        out_specs=P("dp", "tm", "space", None, None),
        check_vma=False,
    )
```
